256 devices in a mesh: layer: 8 (over z_hi, core), latent: 32 (over x, z_lo, y).
Axes of the slice: x: 4, y: 4, z: 8 (z_hi: 4, z_lo: 2; z = z_hi * 2 + z_lo), core: 2. Of those that a mesh axis runs over, the one named last changes fastest.
Arguments:
- ids: int32 [512], replicated, may hold values from 0 to 511
- bank: bfloat16 [512, 10752], P('latent', 'layer'), may hold values from -6 to 6
- enc_weight: bfloat16 [10752, 32768], P('layer', 'latent'), may hold values from -0.0625 to 0.0625
- enc_bias: float32 [32768], P('latent'), may hold values from -3 to 3
- dec_weight: bfloat16 [32768, 10752], P('latent', 'layer'), may hold values from -0.198873782 to 0.198873782
- dec_bias: float32 [10752], P('layer'), may hold values from -3 to 3
Outputs:
- grad_encoder: bfloat16 [10752, 32768], P('layer', 'latent')
- grad_decoder: bfloat16 [32768, 10752], P('latent', 'layer')
The draws below stay inside these ranges and needn't reach their ends.
All inputs are finite; a program needn't handle non-finite values.
Results may differ from the reference program's by a relative error of at most 0.025.
Values may be sent and summed in bfloat16 or wider, within the bound.
A program may use at most 64 MiB of HBM per device.

```python
import math
import jax
import jax.numpy as jnp
from jax import lax

D = 3584
LAYERS = 3
LAT = 32768
TOKENS = 512
FEAT = 10752
BANK = 512


def draw_dec_weight(key, part):
    key = jax.random.fold_in(key, 11)
    first, second, third = jax.random.split(key, 3)
    base = jnp.clip(jax.random.normal(first, (LAT, FEAT), jnp.float32), -6.0, 6.0)
    row_scale = jnp.exp(jax.random.uniform(second, (LAT, 1), jnp.float32, math.log(0.3), math.log(3.0)))
    col_scale = jnp.exp(jax.random.uniform(third, (1, FEAT), jnp.float32, math.log(0.5), math.log(2.0)))
    values = base * row_scale * col_scale * (1.0 / math.sqrt(LAT))
    return values.astype(jnp.bfloat16)


def plant(entries, key, low, high):
    longest = entries.shape.index(max(entries.shape))
    spots = []
    for shift in (0, 1):
        where = [jax.random.randint(jax.random.fold_in(key, axis), (), 0, length) for axis, length in enumerate(entries.shape)]
        where[longest] = (where[longest] + shift) % entries.shape[longest]
        spots.append(tuple(where))
    return entries.at[spots[0]].set(low).at[spots[1]].set(high)


def block_scale(rng, shape, cuts, least, high):
    def one(axis_at, blocks):
        steps = jax.random.uniform(jax.random.fold_in(jax.random.fold_in(rng, 6), axis_at), (blocks,), jnp.float32, least / len(cuts), high / len(cuts))
        return jnp.repeat(jnp.exp(steps), shape[axis_at] // blocks).reshape((-1,) + (1,) * (len(shape) - axis_at - 1))

    level = one(*cuts[0])
    for cut in cuts[1:]:
        level = level * one(*cut)
    return level


def scatter_about(own_key, shape, width, limit, cuts=(), kind=jnp.bfloat16):
    result = jax.random.normal(own_key, shape, jnp.float32) * width
    if len(cuts) > 0:
        result = block_scale(own_key, shape, cuts, -0.22, 0.18) * result
    return jnp.clip(result, min=-limit, max=limit).astype(kind)


def setup_inputs(seed: int = 0) -> dict:
    streams_of = jax.random.split(jax.random.key(seed), 7)
    return {
        "ids": plant(jax.random.randint(streams_of[0], (TOKENS,), 0, BANK), jax.random.fold_in(streams_of[0], 1), 0, BANK - 1).astype(jnp.int32),
        "bank": scatter_about(streams_of[1], (BANK, FEAT), 1.0, 6.0, ((0, 32), (1, 8))),
        "enc_weight": scatter_about(streams_of[2], (FEAT, LAT), FEAT ** -0.5, 0.0625, ((0, 8), (1, 32))),
        "enc_bias": scatter_about(streams_of[3], (LAT,), 0.5, 3.0, ((0, 32),), jnp.float32),
        "dec_weight": draw_dec_weight(jax.random.fold_in(streams_of[6], 71), 0),
        "dec_bias": scatter_about(streams_of[5], (FEAT,), 0.5, 3.0, ((0, 8),), jnp.float32),
    }


penalty_weight = 0.3

def reference(ids, bank, enc_weight, enc_bias, dec_weight, dec_bias):
    inputs = jnp.take(bank, ids, axis=0)
    scale = 1.0 / math.sqrt(TOKENS)
    block = min(LAT, 2048)
    count = LAT // block
    starts = jnp.arange(count, dtype=jnp.int32) * block

    def forward(carry, start):
        w_enc = lax.dynamic_slice_in_dim(enc_weight, start, block, 1)
        w_dec = lax.dynamic_slice_in_dim(dec_weight, start, block, 0)
        bias = lax.dynamic_slice_in_dim(enc_bias, start, block, 0)
        pre = jnp.dot(inputs, w_enc, preferred_element_type=jnp.float32) + bias.astype(jnp.float32)
        latents = jax.nn.softplus(pre).astype(jnp.bfloat16)
        carry = carry + jnp.dot(latents, w_dec, preferred_element_type=jnp.float32)
        wide = w_dec.astype(jnp.float32)
        squares = lax.optimization_barrier(jnp.sum((wide * wide).reshape(block, LAYERS, D), axis=2))
        return (carry, (pre, latents, squares))
    start_sum = jnp.zeros((TOKENS, FEAT), jnp.float32)
    total, (pres, lats, sqs) = lax.scan(forward, start_sum, starts)
    recon = total + dec_bias.astype(jnp.float32)
    resid_grad = ((recon - inputs.astype(jnp.float32)) * scale).astype(jnp.bfloat16)

    def backward(item):
        start, pre, latents, squares = item
        w_dec = lax.dynamic_slice_in_dim(dec_weight, start, block, 0)
        norms = jnp.sqrt(squares + 1e-06)
        total_norm = lax.optimization_barrier(jnp.sum(norms, axis=1))
        latent_grad = lax.dot_general(resid_grad, w_dec, (((1,), (1,)), ((), ())), preferred_element_type=jnp.float32)
        latent_grad = latent_grad + penalty_weight * scale * total_norm[None, :]
        pre_grad = (latent_grad * jax.nn.sigmoid(pre)).astype(jnp.bfloat16)
        g_enc = lax.dot_general(inputs, pre_grad, (((0,), (0,)), ((), ())), preferred_element_type=jnp.float32)
        colsum = lax.optimization_barrier(jnp.sum(latents.astype(jnp.float32), axis=0))
        inverse = jnp.repeat(1.0 / norms, D, axis=1)
        wide = w_dec.astype(jnp.float32)
        g_dec = lax.dot_general(latents, resid_grad, (((0,), (0,)), ((), ())), preferred_element_type=jnp.float32)
        g_dec = g_dec + (penalty_weight * scale * colsum)[:, None] * wide * inverse
        return (g_enc.astype(jnp.bfloat16), g_dec.astype(jnp.bfloat16))
    g_encs, g_decs = lax.map(backward, (starts, pres, lats, sqs))
    grad_encoder = jnp.transpose(g_encs, (1, 0, 2)).reshape(FEAT, LAT)
    grad_decoder = g_decs.reshape(LAT, FEAT)
    return (grad_encoder, grad_decoder)
```

```python
import functools
import math

import jax
import jax.numpy as jnp
from jax import lax
from jax.experimental import pallas as pl
from jax.experimental.pallas import tpu as pltpu
from jax.sharding import PartitionSpec as P

D = 3584
LAYERS = 3
PENALTY = 0.3
ROWS = 16
F0 = 640
CHUNKS = 2
MESH = pl.DeviceIdType.MESH
BF = jnp.bfloat16
F32 = jnp.float32


class Links:
    def __init__(self, send_sems, recv_sems, me):
        self.send_sems, self.recv_sems, self.me = send_sems, recv_sems, me
        self.names, self.pending = {}, []

    def number(self, name):
        return self.names.setdefault(name, len(self.names))

    def copy(self, name, src, dst, device):
        i = self.number(name)
        return pltpu.make_async_remote_copy(
            src_ref=src,
            dst_ref=dst,
            send_sem=self.send_sems.at[i],
            recv_sem=self.recv_sems.at[i],
            device_id=device,
            device_id_type=MESH,
        )

    def send(self, name, src, dst, device):
        copy = self.copy(name, src, dst, device)
        copy.start()
        self.pending.append(copy)

    def recv(self, name, view):
        self.copy(name, view, view, self.me).wait_recv()

    def drain(self):
        for copy in self.pending:
            copy.wait_send()
        self.pending = []


class Ring:
    def __init__(self, place, device_at):
        self.place, self.device_at = place, device_at

    def at(self, shift):
        return lax.rem(self.place + shift % 4, 4)

    def device(self, shift):
        return self.device_at(self.at(shift))


def gather_start(links, tag, ring, view):
    p = ring.at(0)
    links.send((tag, "n0"), view(p, 0), view(p, 0), ring.device(1))
    links.send((tag, "p1"), view(p, 1), view(p, 1), ring.device(-1))
    links.send((tag, "n1"), view(p, 1), view(p, 1), ring.device(1))
    links.send((tag, "p0"), view(p, 0), view(p, 0), ring.device(-1))


def gather_forward(links, tag, ring, view):
    left, right = ring.at(-1), ring.at(1)
    links.recv((tag, "n0"), view(left, 0))
    links.send((tag, "fn"), view(left, 0), view(left, 0), ring.device(1))
    links.recv((tag, "p1"), view(right, 1))
    links.send((tag, "fp"), view(right, 1), view(right, 1), ring.device(-1))


def gather_finish(links, tag, ring, view):
    links.recv((tag, "n1"), view(ring.at(-1), 1))
    links.recv((tag, "p0"), view(ring.at(1), 0))
    links.recv((tag, "fn"), view(ring.at(2), 0))
    links.recv((tag, "fp"), view(ring.at(2), 1))


def scatter_start(links, tag, ring, part, got):
    links.send((tag, "f0"), part(ring.at(2), 0), got(0), ring.device(1))
    links.send((tag, "f1"), part(ring.at(2), 1), got(1), ring.device(-1))
    links.send((tag, "d1"), part(ring.at(1), 1), got(2), ring.device(1))
    links.send((tag, "d0"), part(ring.at(-1), 0), got(3), ring.device(-1))


def scatter_middle(links, tag, ring, part, got, both):
    links.recv((tag, "f0"), got(0))
    both(0)[...] = (part(ring.at(1), 0)[...].astype(F32) + got(0)[...].astype(F32)).astype(BF)
    links.send((tag, "c0"), both(0), got(4), ring.device(1))
    links.recv((tag, "f1"), got(1))
    both(1)[...] = (part(ring.at(-1), 1)[...].astype(F32) + got(1)[...].astype(F32)).astype(BF)
    links.send((tag, "c1"), both(1), got(5), ring.device(-1))


def scatter_finish(links, tag, ring, part, got):
    p = ring.at(0)
    links.recv((tag, "d0"), got(3))
    links.recv((tag, "c0"), got(4))
    first = part(p, 0)[...].astype(F32) + got(3)[...].astype(F32) + got(4)[...].astype(F32)
    links.recv((tag, "d1"), got(2))
    links.recv((tag, "c1"), got(5))
    second = part(p, 1)[...].astype(F32) + got(2)[...].astype(F32) + got(5)[...].astype(F32)
    return first, second


def direct_start(links, tag, ring, source, target):
    for d in (1, 2, 3):
        links.send((tag, d), source(ring.at(d)), target(ring.at(0)), ring.device(d))


def direct_finish(links, tag, ring, target):
    for d in (1, 2, 3):
        links.recv((tag, d), target(ring.at(-d)))


def kernel(
    scale,
    ids_ref, bank_ref, bias_ref, dbias_ref, enc_hbm, dec_hbm,
    bank0_out, bank1_out, lat_out, res0_out, res1_out, pg_out, coef_ref,
    enc, dec, blk0, blk1, bk0, bk1,
    parts, from_core, sums, zgot, zboth, lat, pg, slope,
    rp0, rp1, got0, got1, both0, both1, s0, s1, d0, d1, q0, q1, e0, e1, rs0, rs1,
    sq_part, sq_core, sq_chip, sq_z,
    send_sems, recv_sems, local_sems,
):
    layer, latent = lax.axis_index("layer"), lax.axis_index("latent")
    z, core = layer // 2, lax.rem(layer, 2)
    x, y = latent // 8, lax.rem(latent, 4)
    zl = lax.rem(latent // 4, 2)
    features = enc.shape[0]
    ring_z = Ring(z, lambda q: (q * 2 + core, latent))
    ring_x = Ring(x, lambda q: (layer, q * 8 + zl * 4 + y))
    ring_y = Ring(y, lambda q: (layer, x * 8 + zl * 4 + q))
    core_peer = (z * 2 + 1 - core, latent)
    zl_peer = (layer, x * 8 + (1 - zl) * 4 + y)
    links = Links(send_sems, recv_sems, (layer, latent))

    dec_copy = pltpu.make_async_copy(dec_hbm, dec, local_sems.at[0])
    enc_copy = pltpu.make_async_copy(enc_hbm, enc, local_sems.at[1])
    dec_copy.start()
    enc_copy.start()

    partners = [core_peer, zl_peer]
    for ring in (ring_x, ring_y, ring_z):
        partners += [ring.device(d) for d in (1, 2, 3)]
    barrier = pltpu.get_barrier_semaphore()
    for device in partners:
        pl.semaphore_signal(barrier, inc=1, device_id=device, device_id_type=MESH)
    pl.semaphore_wait(barrier, len(partners))

    def counts(rows):
        hits = (ids_ref[...] == rows).astype(F32)
        return jnp.sum(hits, axis=1, keepdims=True)

    def bank_rows(k, block, n):
        i = lax.broadcasted_iota(jnp.int32, (n, 1), 0)
        b = block + i // ROWS
        return ((b // 4 * 2 + k) * 4 + lax.rem(b, 4)) * ROWS + lax.rem(i, ROWS)

    def x_view(buf, k):
        return lambda q, h: buf.at[k, q, pl.ds(2 * h, 2)]

    def y_view(buf, k):
        return lambda q, h: buf.at[k, pl.ds(2 * h, 2), q]

    def plane_first_start(tag, k, b0, b1):
        direct_start(links, (tag, k, 0), ring_y, lambda q: b0.at[k, x, y], lambda q: b0.at[k, x, q])
        direct_start(links, (tag, k, 1), ring_x, lambda q: b1.at[k, x, y], lambda q: b1.at[k, q, y])

    def plane_first_finish(tag, k, b0, b1):
        direct_finish(links, (tag, k, 0), ring_y, lambda q: b0.at[k, x, q])
        direct_finish(links, (tag, k, 1), ring_x, lambda q: b1.at[k, q, y])

    def plane_second(step, tag, k, b0, b1):
        step(links, (tag, k, "x"), ring_x, x_view(b0, k))
        step(links, (tag, k, "y"), ring_y, y_view(b1, k))

    def z_part(s, k):
        return lambda q, h: sums.at[s, k, q, h]

    def z_got(s, k):
        return lambda i: zgot.at[s, k, i]

    def z_both(s, k):
        return lambda i: zboth.at[s, k, i]

    def z_view(buf, k):
        return lambda q, h: buf.at[k, core, q, h]

    def product_send(s, k):
        links.send(("core", s, k), parts.at[s, k, 1 - core], from_core.at[s, k], core_peer)

    def z_scatter_start(s, k):
        links.recv(("core", s, k), from_core.at[s, k])
        own = parts[s, k, core].astype(F32) + from_core[s, k].astype(F32)
        sums[s, k] = own.astype(BF)
        scatter_start(links, ("zs", s, k), ring_z, z_part(s, k), z_got(s, k))

    def z_scatter_middle(s, k):
        scatter_middle(links, ("zs", s, k), ring_z, z_part(s, k), z_got(s, k), z_both(s, k))

    def z_scatter_finish(s, k):
        return scatter_finish(links, ("zs", s, k), ring_z, z_part(s, k), z_got(s, k))

    def z_gather_start(s, k, buf):
        gather_start(links, ("zg", s, k), ring_z, z_view(buf, k))
        own = buf.at[k, core, z]
        links.send(("zc", s, k, 0), own, own, core_peer)

    def z_gather_forward(s, k, buf):
        gather_forward(links, ("zg", s, k), ring_z, z_view(buf, k))

    def z_gather_finish(s, k, buf):
        view = z_view(buf, k)
        links.recv((("zg", s, k), "n1"), view(ring_z.at(-1), 1))
        block = buf.at[k, core, ring_z.at(-1)]
        links.send(("zc", s, k, 1), block, block, core_peer)
        links.recv((("zg", s, k), "p0"), view(ring_z.at(1), 0))
        block = buf.at[k, core, ring_z.at(1)]
        links.send(("zc", s, k, 2), block, block, core_peer)
        links.recv((("zg", s, k), "fn"), view(ring_z.at(2), 0))
        links.recv((("zg", s, k), "fp"), view(ring_z.at(2), 1))
        block = buf.at[k, core, ring_z.at(2)]
        links.send(("zc", s, k, 3), block, block, core_peer)
        for i, shift in enumerate((0, -1, 1, 2)):
            links.recv(("zc", s, k, i), buf.at[k, 1 - core, ring_z.at(shift)])

    def encode(k):
        b0 = bk0[k].reshape(256, F0)
        b1 = bk1[k].reshape(256, features - F0)

        def tile(n, carry):
            at = pl.ds(pl.multiple_of(n * 256, 256), 256)
            out = jnp.dot(b0, enc[:F0, at], preferred_element_type=F32)
            out += jnp.dot(b1, enc[F0:, at], preferred_element_type=F32)
            parts[0, k, :, :, :, :, at] = out.astype(BF).reshape(2, 4, 2, ROWS, 256)
            return carry

        lax.fori_loop(0, 4, tile, 0)
        product_send(0, k)

    def latents(k):
        halves = z_scatter_finish(0, k)
        for h in (0, 1):
            pre = halves[h] + bias_ref[...]
            soft = jnp.maximum(pre, 0.0) + jnp.log1p(jnp.exp(-jnp.abs(pre)))
            lat[k, core, z, h] = soft.astype(BF)
            slope[k, h] = jax.nn.sigmoid(pre)
        z_gather_start(0, k, lat)

    def decode(k):
        rows = lat[k].reshape(256, 1024)
        out = jnp.dot(rows, dec[:, :F0], preferred_element_type=F32)
        rp0[k] = out.astype(BF).reshape(4, 4, ROWS, F0)
        scatter_start(links, ("xs", k), ring_x, x_view(rp0, k), lambda i: got0.at[k, i])
        out = jnp.dot(rows, dec[:, F0:], preferred_element_type=F32)
        rp1[k] = out.astype(BF).reshape(4, 4, ROWS, features - F0)
        scatter_start(links, ("ys", k), ring_y, y_view(rp1, k), lambda i: got1.at[k, i])

    def recon_middle(k):
        scatter_middle(
            links, ("xs", k), ring_x, x_view(rp0, k), lambda i: got0.at[k, i], lambda i: both0.at[k, i]
        )
        scatter_middle(
            links, ("ys", k), ring_y, y_view(rp1, k), lambda i: got1.at[k, i], lambda i: both1.at[k, i]
        )

    def recon_second(k):
        a, b = scatter_finish(links, ("xs", k), ring_x, x_view(rp0, k), lambda i: got0.at[k, i])
        s0[k, 0:2] = a.astype(BF)
        s0[k, 2:4] = b.astype(BF)
        direct_start(links, ("xt", k), ring_y, lambda q: s0.at[k, q], lambda q: d0.at[k, q])
        a, b = scatter_finish(links, ("ys", k), ring_y, y_view(rp1, k), lambda i: got1.at[k, i])
        s1[k, 0:2] = a.astype(BF)
        s1[k, 2:4] = b.astype(BF)
        direct_start(links, ("yt", k), ring_x, lambda q: s1.at[k, q], lambda q: d1.at[k, q])

    def recon_third(k):
        for tag, ring, s, d, q, e in (("xt", ring_y, s0, d0, q0, e0), ("yt", ring_x, s1, d1, q1, e1)):
            direct_finish(links, (tag, k), ring, lambda j: d.at[k, j])
            total = s[k, ring.at(0)].astype(F32)
            for shift in (1, 2, 3):
                total += d[k, ring.at(shift)].astype(F32)
            q[k] = total.astype(BF)
            links.send((tag, "zl", k), q.at[k], e.at[k], zl_peer)

    def residual(k, own_counts):
        for tag, at, q, e, bk, rs in (
            ("xt", pl.ds(0, F0), q0, e0, bk0, rs0),
            ("yt", pl.ds(F0, features - F0), q1, e1, bk1, rs1),
        ):
            links.recv((tag, "zl", k), e.at[k])
            recon = q[k].astype(F32) + e[k].astype(F32) + dbias_ref[:, at]
            value = (recon - bk[k, x, y].astype(F32)) * scale
            rs[k, x, y] = (value * own_counts).astype(BF)
        plane_first_start("r", k, rs0, rs1)

    def backward(k):
        r0 = rs0[k].reshape(256, F0)
        r1 = rs1[k].reshape(256, features - F0)
        over = (((1,), (1,)), ((), ()))

        def tile(n, carry):
            at = pl.ds(pl.multiple_of(n * 256, 256), 256)
            out = lax.dot_general(r0, dec[at, :F0], over, preferred_element_type=F32)
            out += lax.dot_general(r1, dec[at, F0:], over, preferred_element_type=F32)
            parts[1, k, :, :, :, :, at] = out.astype(BF).reshape(2, 4, 2, ROWS, 256)
            return carry

        lax.fori_loop(0, 4, tile, 0)
        product_send(1, k)

    def latent_gradient(k, row_counts, total_norm):
        halves = z_scatter_finish(1, k)
        for h in (0, 1):
            weight = row_counts[h * ROWS : (h + 1) * ROWS]
            grad = halves[h] + weight * (PENALTY * scale * total_norm)
            pg[k, core, z, h] = (grad * slope[k, h]).astype(BF)
        z_gather_start(1, k, pg)

    blk0[zl] = bank_ref[:, :F0]
    blk1[zl] = bank_ref[:, F0:]
    links.send("bz0", blk0.at[zl], blk0.at[zl], zl_peer)
    links.send("bz1", blk1.at[zl], blk1.at[zl], zl_peer)
    own_counts = [counts(bank_rows(k, x * 4 + y, ROWS)) for k in range(CHUNKS)]
    row_counts = [counts(bank_rows(k, core * 8 + z * 2, 2 * ROWS)) for k in range(CHUNKS)]
    links.recv("bz0", blk0.at[1 - zl])
    links.recv("bz1", blk1.at[1 - zl])
    for k in range(CHUNKS):
        bk0[k, x, y] = blk0[k]
        bk1[k, x, y] = blk1[k]
        plane_first_start("b", k, bk0, bk1)

    dec_copy.wait()
    row = lax.broadcasted_iota(jnp.int32, (8, features), 0)
    column = lax.broadcasted_iota(jnp.int32, (8, features), 1) + layer * features
    owner = jnp.where((column >= row * D) & (column < (row + 1) * D), 1.0, 0.0).astype(BF)

    def square(n, carry):
        at = pl.ds(pl.multiple_of(n * 256, 256), 256)
        wide = dec[at, :].astype(F32)
        wide = wide * wide
        high = wide.astype(BF)
        low = (wide - high.astype(F32)).astype(BF)
        over = (((1,), (1,)), ((), ()))
        total = lax.dot_general(owner, high, over, preferred_element_type=F32)
        total += lax.dot_general(owner, low, over, preferred_element_type=F32)
        sq_part[:, at] = total
        return carry

    lax.fori_loop(0, 4, square, 0)
    links.send("sqc", sq_part, sq_core, core_peer)

    plane_first_finish("b", 0, bk0, bk1)
    plane_second(gather_start, "b2", 0, bk0, bk1)
    links.recv("sqc", sq_core)
    sq_chip[...] = sq_part[...] + sq_core[...]
    direct_start(links, "sqz", ring_z, lambda q: sq_chip, lambda q: sq_z.at[q])
    plane_first_finish("b", 1, bk0, bk1)
    enc_copy.wait()
    plane_second(gather_forward, "b2", 0, bk0, bk1)
    plane_second(gather_start, "b2", 1, bk0, bk1)
    plane_second(gather_finish, "b2", 0, bk0, bk1)
    encode(0)
    plane_second(gather_forward, "b2", 1, bk0, bk1)
    z_scatter_start(0, 0)
    plane_second(gather_finish, "b2", 1, bk0, bk1)
    encode(1)
    z_scatter_middle(0, 0)
    z_scatter_start(0, 1)
    bank0_copy = pltpu.make_async_copy(bk0, bank0_out, local_sems.at[2])
    bank1_copy = pltpu.make_async_copy(bk1, bank1_out, local_sems.at[3])
    bank0_copy.start()
    bank1_copy.start()
    direct_finish(links, "sqz", ring_z, lambda q: sq_z.at[q])
    squares = sq_chip[...]
    for shift in (1, 2, 3):
        squares += sq_z[ring_z.at(shift)]
    norms = jnp.sqrt(squares + 1e-6)
    total_norm = norms[0:1] + norms[1:2] + norms[2:3]
    latents(0)
    z_scatter_middle(0, 1)
    z_gather_forward(0, 0, lat)
    latents(1)
    z_gather_finish(0, 0, lat)
    decode(0)
    z_gather_forward(0, 1, lat)
    recon_middle(0)
    z_gather_finish(0, 1, lat)
    decode(1)
    recon_second(0)
    recon_middle(1)
    recon_third(0)
    lat_copy = pltpu.make_async_copy(lat, lat_out, local_sems.at[4])
    lat_copy.start()
    recon_second(1)
    residual(0, own_counts[0])
    recon_third(1)
    plane_first_finish("r", 0, rs0, rs1)
    plane_second(gather_start, "r2", 0, rs0, rs1)
    residual(1, own_counts[1])
    plane_second(gather_forward, "r2", 0, rs0, rs1)
    plane_first_finish("r", 1, rs0, rs1)
    plane_second(gather_start, "r2", 1, rs0, rs1)
    plane_second(gather_finish, "r2", 0, rs0, rs1)
    backward(0)
    plane_second(gather_forward, "r2", 1, rs0, rs1)
    z_scatter_start(1, 0)
    plane_second(gather_finish, "r2", 1, rs0, rs1)
    backward(1)
    z_scatter_middle(1, 0)
    z_scatter_start(1, 1)
    res0_copy = pltpu.make_async_copy(rs0, res0_out, local_sems.at[5])
    res1_copy = pltpu.make_async_copy(rs1, res1_out, local_sems.at[6])
    res0_copy.start()
    res1_copy.start()
    latent_gradient(0, row_counts[0], total_norm)
    z_scatter_middle(1, 1)
    z_gather_forward(1, 0, pg)
    latent_gradient(1, row_counts[1], total_norm)
    colsum = jnp.zeros((1, 1024), F32)
    for k in range(CHUNKS):
        weight = counts(bank_rows(k, 0, 256))
        colsum += jnp.sum(lat[k].reshape(256, 1024).astype(F32) * weight, axis=0, keepdims=True)
    coef_ref[...] = (PENALTY * scale * colsum) / norms
    z_gather_finish(1, 0, pg)
    z_gather_forward(1, 1, pg)
    z_gather_finish(1, 1, pg)
    pg_copy = pltpu.make_async_copy(pg, pg_out, local_sems.at[7])
    pg_copy.start()
    links.drain()
    for copy in (bank0_copy, bank1_copy, lat_copy, res0_copy, res1_copy, pg_copy):
        copy.wait()


def shards(ids, bank, enc_weight, enc_bias, dec_weight, dec_bias):
    tokens = ids.shape[0]
    features, lats = enc_weight.shape
    f1 = features - F0
    scale = 1.0 / math.sqrt(tokens)
    k = CHUNKS
    vmem = pl.BlockSpec(memory_space=pltpu.VMEM)
    hbm = pl.BlockSpec(memory_space=pl.ANY)
    messages = 256
    bank0, bank1, lat, res0, res1, pg, coef = pl.pallas_call(
        functools.partial(kernel, scale),
        out_shape=[
            jax.ShapeDtypeStruct((k, 4, 4, ROWS, F0), BF),
            jax.ShapeDtypeStruct((k, 4, 4, ROWS, f1), BF),
            jax.ShapeDtypeStruct((k, 2, 4, 2, ROWS, lats), BF),
            jax.ShapeDtypeStruct((k, 4, 4, ROWS, F0), BF),
            jax.ShapeDtypeStruct((k, 4, 4, ROWS, f1), BF),
            jax.ShapeDtypeStruct((k, 2, 4, 2, ROWS, lats), BF),
            jax.ShapeDtypeStruct((8, lats), F32),
        ],
        in_specs=[vmem, vmem, vmem, vmem, hbm, hbm],
        out_specs=[hbm] * 6 + [vmem],
        scratch_shapes=[
            pltpu.VMEM((features, lats), BF),
            pltpu.VMEM((lats, features), BF),
            pltpu.VMEM((2, ROWS, F0), BF),
            pltpu.VMEM((2, ROWS, f1), BF),
            pltpu.VMEM((k, 4, 4, ROWS, F0), BF),
            pltpu.VMEM((k, 4, 4, ROWS, f1), BF),
            pltpu.VMEM((2, k, 2, 4, 2, ROWS, lats), BF),
            pltpu.VMEM((2, k, 4, 2, ROWS, lats), BF),
            pltpu.VMEM((2, k, 4, 2, ROWS, lats), BF),
            pltpu.VMEM((2, k, 6, ROWS, lats), BF),
            pltpu.VMEM((2, k, 2, ROWS, lats), BF),
            pltpu.VMEM((k, 2, 4, 2, ROWS, lats), BF),
            pltpu.VMEM((k, 2, 4, 2, ROWS, lats), BF),
            pltpu.VMEM((k, 2, ROWS, lats), F32),
            pltpu.VMEM((k, 4, 4, ROWS, F0), BF),
            pltpu.VMEM((k, 4, 4, ROWS, f1), BF),
            pltpu.VMEM((k, 6, 2, ROWS, F0), BF),
            pltpu.VMEM((k, 6, 2, ROWS, f1), BF),
            pltpu.VMEM((k, 2, 2, ROWS, F0), BF),
            pltpu.VMEM((k, 2, 2, ROWS, f1), BF),
            pltpu.VMEM((k, 4, ROWS, F0), BF),
            pltpu.VMEM((k, 4, ROWS, f1), BF),
            pltpu.VMEM((k, 4, ROWS, F0), BF),
            pltpu.VMEM((k, 4, ROWS, f1), BF),
            pltpu.VMEM((k, ROWS, F0), BF),
            pltpu.VMEM((k, ROWS, f1), BF),
            pltpu.VMEM((k, ROWS, F0), BF),
            pltpu.VMEM((k, ROWS, f1), BF),
            pltpu.VMEM((k, 4, 4, ROWS, F0), BF),
            pltpu.VMEM((k, 4, 4, ROWS, f1), BF),
            pltpu.VMEM((8, lats), F32),
            pltpu.VMEM((8, lats), F32),
            pltpu.VMEM((8, lats), F32),
            pltpu.VMEM((4, 8, lats), F32),
            pltpu.SemaphoreType.DMA((messages,)),
            pltpu.SemaphoreType.DMA((messages,)),
            pltpu.SemaphoreType.DMA((8,)),
        ],
        compiler_params=pltpu.CompilerParams(
            collective_id=0, has_side_effects=True, vmem_limit_bytes=56 * 2**20
        ),
        name="crosscoder_step",
    )(ids[None, :], bank, enc_bias[None, :], dec_bias[None, :], enc_weight, dec_weight)

    inputs = jnp.concatenate([bank0.reshape(-1, F0), bank1.reshape(-1, f1)], axis=1)
    resid = jnp.concatenate([res0.reshape(-1, F0), res1.reshape(-1, f1)], axis=1)
    over = (((0,), (0,)), ((), ()))
    grad_encoder = lax.dot_general(inputs, pg.reshape(-1, lats), over, preferred_element_type=F32)
    grad_decoder = lax.dot_general(lat.reshape(-1, lats), resid, over, preferred_element_type=F32)
    feature = lax.axis_index("layer") * features + lax.iota(jnp.int32, features)
    owner = (feature // D)[None, :]
    factor = coef.T
    spread = jnp.where(owner == 0, factor[:, 0:1], jnp.where(owner == 1, factor[:, 1:2], factor[:, 2:3]))
    grad_decoder = grad_decoder + spread * dec_weight.astype(F32)
    return (grad_encoder.astype(BF), grad_decoder.astype(BF))


def solution(mesh):
    in_specs = (
        P(),
        P("latent", "layer"),
        P("layer", "latent"),
        P("latent"),
        P("latent", "layer"),
        P("layer"),
    )
    out_specs = (P("layer", "latent"), P("latent", "layer"))
    return jax.shard_map(shards, mesh=mesh, in_specs=in_specs, out_specs=out_specs, check_vma=False)
```

```python
import functools
import math

import jax
import jax.numpy as jnp
from jax import lax
from jax.experimental import pallas as pl
from jax.experimental.pallas import tpu as pltpu
from jax.sharding import PartitionSpec as P

D = 3584
LAYERS = 3
PENALTY = 0.3
ROWS = 16
F0 = 640
CHUNKS = 2
MESH = pl.DeviceIdType.MESH
BF = jnp.bfloat16
F32 = jnp.float32


class Links:
    def __init__(self, send_sems, recv_sems, me):
        self.send_sems, self.recv_sems, self.me = send_sems, recv_sems, me
        self.names, self.families = {}, {}

    def copy(self, name, src, dst, device):
        i = self.names.setdefault(name, len(self.names))
        j = self.families.setdefault(name[0], len(self.families))
        return pltpu.make_async_remote_copy(
            src_ref=src,
            dst_ref=dst,
            send_sem=self.send_sems.at[j],
            recv_sem=self.recv_sems.at[i],
            device_id=device,
            device_id_type=MESH,
        )

    def send(self, name, src, dst, device):
        self.copy(name, src, dst, device).start()

    def recv(self, name, view):
        self.copy(name, view, view, self.me).wait_recv()

    def sent(self, family, view):
        i = self.families[family]
        pltpu.make_async_copy(view, view, self.send_sems.at[i]).wait()


class Ring:
    def __init__(self, place, device_at):
        self.place, self.device_at = place, device_at

    def at(self, shift):
        return lax.rem(self.place + shift % 4, 4)

    def device(self, shift):
        return self.device_at(self.at(shift))


def gather_start(links, tag, ring, view):
    p = ring.at(0)
    links.send((*tag, "n0"), view(p, 0), view(p, 0), ring.device(1))
    links.send((*tag, "p1"), view(p, 1), view(p, 1), ring.device(-1))
    links.send((*tag, "own"), view(p, 1), view(p, 1), ring.device(1))
    links.send((*tag, "own"), view(p, 0), view(p, 0), ring.device(-1))


def gather_forward(links, tag, ring, view):
    left, right = ring.at(-1), ring.at(1)
    links.recv((*tag, "n0"), view(left, 0))
    links.send((*tag, "far"), view(left, 0), view(left, 0), ring.device(1))
    links.recv((*tag, "p1"), view(right, 1))
    links.send((*tag, "far"), view(right, 1), view(right, 1), ring.device(-1))


def scatter_start(links, tag, ring, part, got):
    links.send((*tag, "f0"), part(ring.at(2), 0), got(0), ring.device(1))
    links.send((*tag, "f1"), part(ring.at(2), 1), got(1), ring.device(-1))
    links.send((*tag, "end"), part(ring.at(1), 1), got(2), ring.device(1))
    links.send((*tag, "end"), part(ring.at(-1), 0), got(3), ring.device(-1))


def scatter_middle(links, tag, ring, part, got, both):
    links.recv((*tag, "f0"), got(0))
    both(0)[...] = (part(ring.at(1), 0)[...].astype(F32) + got(0)[...].astype(F32)).astype(BF)
    links.send((*tag, "end"), both(0), got(4), ring.device(1))
    links.recv((*tag, "f1"), got(1))
    both(1)[...] = (part(ring.at(-1), 1)[...].astype(F32) + got(1)[...].astype(F32)).astype(BF)
    links.send((*tag, "end"), both(1), got(5), ring.device(-1))


def scatter_finish(links, tag, ring, part, got, last_four):
    p = ring.at(0)
    links.recv((*tag, "end"), last_four)
    first = part(p, 0)[...].astype(F32) + got(3)[...].astype(F32) + got(4)[...].astype(F32)
    second = part(p, 1)[...].astype(F32) + got(2)[...].astype(F32) + got(5)[...].astype(F32)
    return first, second


def direct_start(links, tag, ring, source, target):
    for d in (2, 1, 3):
        links.send(tag, source(ring.at(d)), target(ring.at(0)), ring.device(d))


def kernel(
    scale,
    ids_ref, bank_ref, bias_ref, dbias_ref, enc_hbm, dec_hbm,
    bank0_out, bank1_out, lat_out, res0_out, res1_out, pg_out, coef_ref,
    enc, dec, blk0, blk1, bk0, bk1,
    parts, from_core, sums, zgot, zboth, lat, pg, slope,
    rp0, rp1, got0, got1, s0, s1, d0, d1, q0, q1, e0, e1, rs0, rs1,
    sq_part, sq_core, sq_chip, sq_z, norms_ref,
    send_sems, recv_sems, local_sems,
):
    layer, latent = lax.axis_index("layer"), lax.axis_index("latent")
    z, core = layer // 2, lax.rem(layer, 2)
    x, y = latent // 8, lax.rem(latent, 4)
    zl = lax.rem(latent // 4, 2)
    features = enc.shape[0]
    ring_z = Ring(z, lambda q: (q * 2 + core, latent))
    ring_x = Ring(x, lambda q: (layer, q * 8 + zl * 4 + y))
    ring_y = Ring(y, lambda q: (layer, x * 8 + zl * 4 + q))
    core_peer = (z * 2 + 1 - core, latent)
    zl_peer = (layer, x * 8 + (1 - zl) * 4 + y)
    links = Links(send_sems, recv_sems, (layer, latent))

    dec_copy = pltpu.make_async_copy(dec_hbm, dec, local_sems.at[0])
    enc_copy = pltpu.make_async_copy(enc_hbm, enc, local_sems.at[1])
    dec_copy.start()
    enc_copy.start()

    partners = [core_peer, zl_peer]
    for ring in (ring_x, ring_y, ring_z):
        partners += [ring.device(d) for d in (1, 2, 3)]
    barrier = pltpu.get_barrier_semaphore()
    for device in partners:
        pl.semaphore_signal(barrier, inc=1, device_id=device, device_id_type=MESH)
    pl.semaphore_wait(barrier, len(partners))

    def counts(rows):
        hits = (ids_ref[...][None, :] == rows).astype(F32)
        return jnp.sum(hits, axis=1, keepdims=True)

    def bank_rows(k, block, n):
        i = lax.broadcasted_iota(jnp.int32, (n, 1), 0)
        b = block + i // ROWS
        return ((b // 4 * 2 + k) * 4 + lax.rem(b, 4)) * ROWS + lax.rem(i, ROWS)

    def plane_first_start(tag, k, b0, b1):
        own = b0.at[k, x, y]
        direct_start(links, (tag + "0", k), ring_y, lambda q: own, lambda q: b0.at[k, x, q])
        own = b1.at[k, x, y]
        direct_start(links, (tag + "1", k), ring_x, lambda q: own, lambda q: b1.at[k, q, y])

    def plane_second_start(tag, k, b0, b1):
        links.recv((tag + "0", k), b0.at[k, x, pl.ds(0, 3)])
        own = b0.at[k, x]
        direct_start(links, (tag + "2", k), ring_x, lambda q: own, lambda q: b0.at[k, q])
        links.recv((tag + "1", k), b1.at[k, pl.ds(0, 3), y])
        block = b1.at[k, :, y]
        direct_start(links, (tag + "3", k), ring_y, lambda q: block, lambda q: b1.at[k, :, q])

    def plane_finish(tag, k, b0, b1):
        links.recv((tag + "2", k), b0.at[k, pl.ds(0, 3)])
        links.recv((tag + "3", k), b1.at[k, pl.ds(0, 3)])

    def z_part(s, k):
        return lambda q, h: sums.at[s, k, q, h]

    def z_got(s, k):
        return lambda i: zgot.at[s, k, i]

    def z_both(s, k):
        return lambda i: zboth.at[s, k, i]

    def z_view(buf, k):
        return lambda q, h: buf.at[k, core, q, h]

    def product_send(s, k):
        links.send(("core", s, k), parts.at[s, k, 1 - core], from_core.at[s, k], core_peer)

    def z_scatter_start(s, k):
        links.recv(("core", s, k), from_core.at[s, k])
        own = parts[s, k, core].astype(F32) + from_core[s, k].astype(F32)
        sums[s, k] = own.astype(BF)
        scatter_start(links, ("zs", s, k), ring_z, z_part(s, k), z_got(s, k))

    def z_scatter_middle(s, k):
        scatter_middle(links, ("zs", s, k), ring_z, z_part(s, k), z_got(s, k), z_both(s, k))

    def z_scatter_finish(s, k):
        last_four = zgot.at[s, k, pl.ds(2, 4)]
        return scatter_finish(links, ("zs", s, k), ring_z, z_part(s, k), z_got(s, k), last_four)

    def to_core(s, k, buf, shift):
        block = buf.at[k, core, ring_z.at(shift)]
        links.send(("zc", s, k), block, block, core_peer)

    def z_gather_start(s, k, buf):
        gather_start(links, ("zg", s, k), ring_z, z_view(buf, k))
        to_core(s, k, buf, 0)

    def z_gather_forward(s, k, buf):
        gather_forward(links, ("zg", s, k), ring_z, z_view(buf, k))

    def z_gather_finish(s, k, buf):
        two = buf.at[k, core, 0]
        links.recv(("zg", s, k, "own"), two)
        to_core(s, k, buf, -1)
        to_core(s, k, buf, 1)
        links.recv(("zg", s, k, "far"), two)
        to_core(s, k, buf, 2)
        links.recv(("zc", s, k), buf.at[k, 1 - core])

    def encode(k):
        b0 = bk0[k].reshape(256, F0)
        b1 = bk1[k].reshape(256, features - F0)

        def tile(n, carry):
            at = pl.ds(pl.multiple_of(n * 256, 256), 256)
            out = jnp.dot(b0, enc[:F0, at], preferred_element_type=F32)
            out += jnp.dot(b1, enc[F0:, at], preferred_element_type=F32)
            parts[0, k, :, :, :, :, at] = out.astype(BF).reshape(2, 4, 2, ROWS, 256)
            return carry

        lax.fori_loop(0, 4, tile, 0)
        product_send(0, k)

    def latents(k):
        halves = z_scatter_finish(0, k)
        for h in (0, 1):
            pre = halves[h] + bias_ref[...][None, :]
            soft = jnp.maximum(pre, 0.0) + jnp.log1p(jnp.exp(-jnp.abs(pre)))
            lat[k, core, z, h] = soft.astype(BF)
            slope[k, h] = jax.nn.sigmoid(pre)
        z_gather_start(0, k, lat)

    def decode(k):
        rows = lat[k].reshape(256, -1)
        over = (((1,), (1,)), ((), ()))
        out = lax.dot_general(rows, dec[:F0], over, preferred_element_type=F32)
        rp0[k] = out.astype(BF).reshape(4, 4, ROWS, F0)
        direct_start(links, ("xs", k), ring_x, lambda q: rp0.at[k, q], lambda q: got0.at[k, q])
        out = lax.dot_general(rows, dec[F0:], over, preferred_element_type=F32)
        rp1[k] = out.astype(BF).reshape(4, 4, ROWS, features - F0)
        direct_start(links, ("ys", k), ring_y, lambda q: rp1.at[k, :, q], lambda q: got1.at[k, q])

    def recon_second(k):
        links.recv(("xs", k), got0.at[k, pl.ds(0, 3)])
        total = rp0[k, x].astype(F32)
        for shift in (1, 2, 3):
            total += got0[k, ring_x.at(shift)].astype(F32)
        s0[k] = total.astype(BF)
        direct_start(links, ("xt", k), ring_y, lambda q: s0.at[k, q], lambda q: d0.at[k, q])
        links.recv(("ys", k), got1.at[k, pl.ds(0, 3)])
        total = rp1[k, :, y].astype(F32)
        for shift in (1, 2, 3):
            total += got1[k, ring_y.at(shift)].astype(F32)
        s1[k] = total.astype(BF)
        direct_start(links, ("yt", k), ring_x, lambda q: s1.at[k, q], lambda q: d1.at[k, q])

    def recon_third(k):
        for tag, ring, s, d, q, e in (("xt", ring_y, s0, d0, q0, e0), ("yt", ring_x, s1, d1, q1, e1)):
            links.recv((tag, k), d.at[k, pl.ds(0, 3)])
            total = s[k, ring.at(0)].astype(F32)
            for shift in (1, 2, 3):
                total += d[k, ring.at(shift)].astype(F32)
            q[k] = total.astype(BF)
            links.send((tag + "z", k), q.at[k], e.at[k], zl_peer)

    def residual(k):
        own_counts = counts(bank_rows(k, x * 4 + y, ROWS))
        for tag, at, q, e, bk, rs in (
            ("xt", pl.ds(0, F0), q0, e0, bk0, rs0),
            ("yt", pl.ds(F0, features - F0), q1, e1, bk1, rs1),
        ):
            links.recv((tag + "z", k), e.at[k])
            recon = q[k].astype(F32) + e[k].astype(F32) + dbias_ref[at][None, :]
            value = (recon - bk[k, x, y].astype(F32)) * scale
            rs[k, x, y] = (value * own_counts).astype(BF)
        plane_first_start("r", k, rs0, rs1)

    def backward(k):
        r0 = rs0[k].reshape(256, F0)
        r1 = rs1[k].reshape(256, features - F0)

        def tile(n, carry):
            at = pl.ds(pl.multiple_of(n * 256, 256), 256)
            out = jnp.dot(r0, dec[:F0, at], preferred_element_type=F32)
            out += jnp.dot(r1, dec[F0:, at], preferred_element_type=F32)
            parts[1, k, :, :, :, :, at] = out.astype(BF).reshape(2, 4, 2, ROWS, 256)
            return carry

        lax.fori_loop(0, 4, tile, 0)
        product_send(1, k)

    def latent_gradient(k):
        row_counts = counts(bank_rows(k, core * 8 + z * 2, 2 * ROWS))
        total_norm = norms_ref[0:1] + norms_ref[1:2] + norms_ref[2:3]
        halves = z_scatter_finish(1, k)
        for h in (0, 1):
            weight = row_counts[h * ROWS : (h + 1) * ROWS]
            grad = halves[h] + weight * (PENALTY * scale * total_norm)
            pg[k, core, z, h] = (grad * slope[k, h]).astype(BF)
        z_gather_start(1, k, pg)

    def bank_send():
        blk0[zl] = bank_ref[:, :F0]
        blk1[zl] = bank_ref[:, F0:]
        links.send(("bz0",), blk0.at[zl], blk0.at[zl], zl_peer)
        links.send(("bz1",), blk1.at[zl], blk1.at[zl], zl_peer)

    def bank_recv():
        links.recv(("bz0",), blk0.at[1 - zl])
        links.recv(("bz1",), blk1.at[1 - zl])
        for k in range(CHUNKS):
            bk0[k, x, y] = blk0[k]
            bk1[k, x, y] = blk1[k]
            plane_first_start("b", k, bk0, bk1)

    def squares_send():
        dec_copy.wait()
        row = lax.broadcasted_iota(jnp.int32, (8, features), 0)
        column = lax.broadcasted_iota(jnp.int32, (8, features), 1) + layer * features
        owner = jnp.where((column >= row * D) & (column < (row + 1) * D), 1.0, 0.0).astype(BF)

        def square(n, carry):
            at = pl.ds(pl.multiple_of(n * 256, 256), 256)
            wide = dec[:, at].astype(F32)
            wide = wide * wide
            high = wide.astype(BF)
            low = (wide - high.astype(F32)).astype(BF)
            total = jnp.dot(owner, high, preferred_element_type=F32)
            total += jnp.dot(owner, low, preferred_element_type=F32)
            sq_part[:, at] = total
            return carry

        lax.fori_loop(0, 4, square, 0)
        links.send(("sqc",), sq_part, sq_core, core_peer)

    def squares_second():
        links.recv(("sqc",), sq_core)
        sq_chip[...] = sq_part[...] + sq_core[...]
        direct_start(links, ("sqz",), ring_z, lambda q: sq_chip, lambda q: sq_z.at[q])

    def squares_sum():
        links.recv(("sqz",), sq_z.at[pl.ds(0, 3)])
        squares = sq_chip[...]
        for shift in (1, 2, 3):
            squares += sq_z[ring_z.at(shift)]
        norms_ref[...] = jnp.sqrt(squares + 1e-6)

    def copy_out(i, src, dst):
        copy = pltpu.make_async_copy(src, dst, local_sems.at[i])
        copy.start()
        outgoing.append(copy)

    def coefficients():
        colsum = jnp.zeros((1, lat.shape[-1]), F32)
        for k in range(CHUNKS):
            weight = counts(bank_rows(k, 0, 256))
            colsum += jnp.sum(lat[k].reshape(256, -1).astype(F32) * weight, axis=0, keepdims=True)
        coef_ref[...] = (PENALTY * scale * colsum) / norms_ref[...]

    outgoing = []
    bank, resid = (bk0, bk1), (rs0, rs1)
    steps = [
        (bank_send,),
        (bank_recv,),
        (squares_send,),
        (plane_second_start, "b", 0, *bank),
        (squares_second,),
        (plane_second_start, "b", 1, *bank),
        (enc_copy.wait,),
        (plane_finish, "b", 0, *bank),
        (encode, 0),
        (z_scatter_start, 0, 0),
        (plane_finish, "b", 1, *bank),
        (encode, 1),
        (z_scatter_middle, 0, 0),
        (z_scatter_start, 0, 1),
        (copy_out, 2, bk0, bank0_out),
        (copy_out, 3, bk1, bank1_out),
        (squares_sum,),
        (latents, 0),
        (z_scatter_middle, 0, 1),
        (z_gather_forward, 0, 0, lat),
        (latents, 1),
        (z_gather_finish, 0, 0, lat),
        (decode, 0),
        (z_gather_forward, 0, 1, lat),
        (z_gather_finish, 0, 1, lat),
        (decode, 1),
        (recon_second, 0),
        (recon_third, 0),
        (recon_second, 1),
        (residual, 0),
        (recon_third, 1),
        (plane_second_start, "r", 0, *resid),
        (residual, 1),
        (copy_out, 4, lat, lat_out),
        (plane_second_start, "r", 1, *resid),
        (plane_finish, "r", 0, *resid),
        (backward, 0),
        (z_scatter_start, 1, 0),
        (plane_finish, "r", 1, *resid),
        (backward, 1),
        (z_scatter_middle, 1, 0),
        (z_scatter_start, 1, 1),
        (copy_out, 5, rs0, res0_out),
        (copy_out, 6, rs1, res1_out),
        (latent_gradient, 0),
        (z_scatter_middle, 1, 1),
        (z_gather_forward, 1, 0, pg),
        (latent_gradient, 1),
        (coefficients,),
        (z_gather_finish, 1, 0, pg),
        (z_gather_forward, 1, 1, pg),
        (z_gather_finish, 1, 1, pg),
        (copy_out, 7, pg, pg_out),
    ]
    for step, *given in steps:
        step(*given)
    for family, view in (
        ("bz0", blk0.at[0]),
        ("bz1", blk1.at[0]),
        ("b0", s0.at[:, pl.ds(0, 3)]),
        ("b1", s1.at[:, pl.ds(0, 3)]),
        ("b2", got0.at[:, pl.ds(0, 3)]),
        ("b3", got1.at[:, pl.ds(0, 3)]),
        ("sqc", sq_part),
        ("sqz", sq_z.at[pl.ds(0, 3)]),
        ("core", sums),
        ("zs", zgot),
        ("zg", zgot),
        ("zc", sums),
        ("xs", got0.at[:, pl.ds(0, 3)]),
        ("ys", got1.at[:, pl.ds(0, 3)]),
        ("xt", s0.at[:, pl.ds(0, 3)]),
        ("yt", s1.at[:, pl.ds(0, 3)]),
        ("xtz", q0),
        ("ytz", q1),
        ("r0", s0.at[:, pl.ds(0, 3)]),
        ("r1", s1.at[:, pl.ds(0, 3)]),
        ("r2", got0.at[:, pl.ds(0, 3)]),
        ("r3", got1.at[:, pl.ds(0, 3)]),
    ):
        links.sent(family, view)
    for copy in outgoing:
        copy.wait()


def shards(ids, bank, enc_weight, enc_bias, dec_weight, dec_bias):
    tokens = ids.shape[0]
    features, lats = enc_weight.shape
    dec = dec_weight.T
    f1 = features - F0
    scale = 1.0 / math.sqrt(tokens)
    k = CHUNKS
    vmem = pl.BlockSpec(memory_space=pltpu.VMEM)
    hbm = pl.BlockSpec(memory_space=pl.ANY)
    messages = 68
    bank0, bank1, lat, res0, res1, pg, coef = pl.pallas_call(
        functools.partial(kernel, scale),
        out_shape=[
            jax.ShapeDtypeStruct((k, 4, 4, ROWS, F0), BF),
            jax.ShapeDtypeStruct((k, 4, 4, ROWS, f1), BF),
            jax.ShapeDtypeStruct((k, 2, 4, 2, ROWS, lats), BF),
            jax.ShapeDtypeStruct((k, 4, 4, ROWS, F0), BF),
            jax.ShapeDtypeStruct((k, 4, 4, ROWS, f1), BF),
            jax.ShapeDtypeStruct((k, 2, 4, 2, ROWS, lats), BF),
            jax.ShapeDtypeStruct((8, lats), F32),
        ],
        in_specs=[vmem, vmem, vmem, vmem, hbm, hbm],
        out_specs=[hbm] * 6 + [vmem],
        scratch_shapes=[
            pltpu.VMEM((features, lats), BF),
            pltpu.VMEM((features, lats), BF),
            pltpu.VMEM((2, ROWS, F0), BF),
            pltpu.VMEM((2, ROWS, f1), BF),
            pltpu.VMEM((k, 4, 4, ROWS, F0), BF),
            pltpu.VMEM((k, 4, 4, ROWS, f1), BF),
            pltpu.VMEM((2, k, 2, 4, 2, ROWS, lats), BF),
            pltpu.VMEM((2, k, 4, 2, ROWS, lats), BF),
            pltpu.VMEM((2, k, 4, 2, ROWS, lats), BF),
            pltpu.VMEM((2, k, 6, ROWS, lats), BF),
            pltpu.VMEM((2, k, 2, ROWS, lats), BF),
            pltpu.VMEM((k, 2, 4, 2, ROWS, lats), BF),
            pltpu.VMEM((k, 2, 4, 2, ROWS, lats), BF),
            pltpu.VMEM((k, 2, ROWS, lats), F32),
            pltpu.VMEM((k, 4, 4, ROWS, F0), BF),
            pltpu.VMEM((k, 4, 4, ROWS, f1), BF),
            pltpu.VMEM((k, 4, 4, ROWS, F0), BF),
            pltpu.VMEM((k, 4, 4, ROWS, f1), BF),
            pltpu.VMEM((k, 4, ROWS, F0), BF),
            pltpu.VMEM((k, 4, ROWS, f1), BF),
            pltpu.VMEM((k, 4, ROWS, F0), BF),
            pltpu.VMEM((k, 4, ROWS, f1), BF),
            pltpu.VMEM((k, ROWS, F0), BF),
            pltpu.VMEM((k, ROWS, f1), BF),
            pltpu.VMEM((k, ROWS, F0), BF),
            pltpu.VMEM((k, ROWS, f1), BF),
            pltpu.VMEM((k, 4, 4, ROWS, F0), BF),
            pltpu.VMEM((k, 4, 4, ROWS, f1), BF),
            pltpu.VMEM((8, lats), F32),
            pltpu.VMEM((8, lats), F32),
            pltpu.VMEM((8, lats), F32),
            pltpu.VMEM((4, 8, lats), F32),
            pltpu.VMEM((8, lats), F32),
            pltpu.SemaphoreType.DMA((22,)),
            pltpu.SemaphoreType.DMA((messages,)),
            pltpu.SemaphoreType.DMA((8,)),
        ],
        compiler_params=pltpu.CompilerParams(
            collective_id=0, has_side_effects=True, vmem_limit_bytes=56 * 2**20
        ),
        name="crosscoder_step",
    )(ids, bank, enc_bias, dec_bias, enc_weight, dec)

    grad_encoder, grad_decoder = gradients(bank0, bank1, res0, res1, lat, pg, coef, dec)
    return grad_encoder, grad_decoder.T


def gradients_kernel(bank0, bank1, res0, res1, lat, pg, coef, dec, enc_grad, dec_grad):
    features = enc_grad.shape[0]
    over = (((0,), (0,)), ((), ()))
    rows = lat.shape[0]
    start = lax.axis_index("layer") * features
    for at, bank, res in ((0, bank0, res0), (F0, bank1, res1)):
        size = bank.shape[-1]
        span = pl.ds(at, size)
        right = lat[...]
        out = lax.dot_general(res[...], right, over, preferred_element_type=F32)
        feature = start + at + lax.broadcasted_iota(jnp.int32, (size, 1), 0)
        spread = jnp.where(
            feature < D, coef[0:1], jnp.where(feature < 2 * D, coef[1:2], coef[2:3])
        )
        dec_grad[span] = (out + spread * dec[span].astype(F32)).astype(BF)
        out = lax.dot_general(bank[...], pg[...], over, preferred_element_type=F32)
        enc_grad[span] = out.astype(BF)


def gradients(bank0, bank1, res0, res1, lat, pg, coef, dec):
    features, lats = dec.shape
    tile = 256
    whole = lambda a: pl.BlockSpec((a.shape[0], a.shape[1]), lambda n: (0, 0))
    piece = lambda a: pl.BlockSpec((a.shape[0], tile), lambda n: (0, n))
    bank0, bank1, res0, res1 = (a.reshape(-1, a.shape[-1]) for a in (bank0, bank1, res0, res1))
    lat, pg = lat.reshape(-1, lats), pg.reshape(-1, lats)
    out = jax.ShapeDtypeStruct((features, lats), BF)
    return pl.pallas_call(
        gradients_kernel,
        out_shape=[out, out],
        grid=(lats // tile,),
        in_specs=[whole(a) for a in (bank0, bank1, res0, res1)]
        + [piece(a) for a in (lat, pg, coef, dec)],
        out_specs=[piece(out), piece(out)],
        compiler_params=pltpu.CompilerParams(vmem_limit_bytes=56 * 2**20),
        name="gradients",
    )(bank0, bank1, res0, res1, lat, pg, coef, dec)


def solution(mesh):
    in_specs = (
        P(),
        P("latent", "layer"),
        P("layer", "latent"),
        P("latent"),
        P("latent", "layer"),
        P("layer"),
    )
    out_specs = (P("layer", "latent"), P("latent", "layer"))
    return jax.shard_map(shards, mesh=mesh, in_specs=in_specs, out_specs=out_specs, check_vma=False)
```

```python
import functools
import math

import jax
import jax.numpy as jnp
from jax import lax
from jax.experimental import pallas as pl
from jax.experimental.pallas import tpu as pltpu
from jax.sharding import PartitionSpec as P

D = 3584
LAYERS = 3
PENALTY = 0.3
ROWS = 16
F0 = 640
CHUNKS = 2
Z_RS = "ring"
Z_AG = "ring"
MESH = pl.DeviceIdType.MESH
BF = jnp.bfloat16
F32 = jnp.float32


class Links:
    def __init__(self, send_sems, recv_sems, me):
        self.send_sems, self.recv_sems, self.me = send_sems, recv_sems, me
        self.names, self.families = {}, {}

    def copy(self, name, src, dst, device):
        i = self.names.setdefault(name, len(self.names))
        j = self.families.setdefault(name[0], len(self.families))
        return pltpu.make_async_remote_copy(
            src_ref=src,
            dst_ref=dst,
            send_sem=self.send_sems.at[j],
            recv_sem=self.recv_sems.at[i],
            device_id=device,
            device_id_type=MESH,
        )

    def send(self, name, src, dst, device):
        self.copy(name, src, dst, device).start()

    def recv(self, name, view):
        self.copy(name, view, view, self.me).wait_recv()

    def sent(self, family, view):
        i = self.families[family]
        pltpu.make_async_copy(view, view, self.send_sems.at[i]).wait()


class Ring:
    def __init__(self, place, device_at):
        self.place, self.device_at = place, device_at

    def at(self, shift):
        return lax.rem(self.place + shift % 4, 4)

    def device(self, shift):
        return self.device_at(self.at(shift))


def gather_start(links, tag, ring, view):
    p = ring.at(0)
    links.send((*tag, "n0"), view(p, 0), view(p, 0), ring.device(1))
    links.send((*tag, "p1"), view(p, 1), view(p, 1), ring.device(-1))
    links.send((*tag, "own"), view(p, 1), view(p, 1), ring.device(1))
    links.send((*tag, "own"), view(p, 0), view(p, 0), ring.device(-1))


def gather_forward(links, tag, ring, view):
    left, right = ring.at(-1), ring.at(1)
    links.recv((*tag, "n0"), view(left, 0))
    links.send((*tag, "far"), view(left, 0), view(left, 0), ring.device(1))
    links.recv((*tag, "p1"), view(right, 1))
    links.send((*tag, "far"), view(right, 1), view(right, 1), ring.device(-1))


def scatter_start(links, tag, ring, part, got):
    links.send((*tag, "f0"), part(ring.at(2), 0), got(0), ring.device(1))
    links.send((*tag, "f1"), part(ring.at(2), 1), got(1), ring.device(-1))
    links.send((*tag, "end"), part(ring.at(1), 1), got(2), ring.device(1))
    links.send((*tag, "end"), part(ring.at(-1), 0), got(3), ring.device(-1))


def scatter_middle(links, tag, ring, part, got, both):
    links.recv((*tag, "f0"), got(0))
    both(0)[...] = (part(ring.at(1), 0)[...].astype(F32) + got(0)[...].astype(F32)).astype(BF)
    links.send((*tag, "end"), both(0), got(4), ring.device(1))
    links.recv((*tag, "f1"), got(1))
    both(1)[...] = (part(ring.at(-1), 1)[...].astype(F32) + got(1)[...].astype(F32)).astype(BF)
    links.send((*tag, "end"), both(1), got(5), ring.device(-1))


def scatter_finish(links, tag, ring, part, got, last_four):
    p = ring.at(0)
    links.recv((*tag, "end"), last_four)
    first = part(p, 0)[...].astype(F32) + got(3)[...].astype(F32) + got(4)[...].astype(F32)
    second = part(p, 1)[...].astype(F32) + got(2)[...].astype(F32) + got(5)[...].astype(F32)
    return first, second


def direct_start(links, tag, ring, source, target):
    for d in (2, 1, 3):
        links.send(tag, source(ring.at(d)), target(ring.at(0)), ring.device(d))


def kernel(
    scale,
    ids_hbm, bank_hbm, bias_hbm, dbias_hbm, enc_hbm, dec_hbm,
    turned_out, dgrad_out, pg_out,
    ids_ref, bank_ref, bias_ref, dbias_ref, enc, dec, blk0, blk1, bk0, bk1,
    parts, from_core, sums, zgot, zboth, lat, pg, slope,
    rp0, rp1, got0, got1, s0, s1, d0, d1, q0, q1, e0, e1, rs0, rs1,
    sq_part, sq_core, sq_chip, sq_z, norms_ref, coef_ref, turned, resid_turned, dgrad,
    send_sems, recv_sems, local_sems,
):
    layer, latent = lax.axis_index("layer"), lax.axis_index("latent")
    z, core = layer // 2, lax.rem(layer, 2)
    x, y = latent // 8, lax.rem(latent, 4)
    zl = lax.rem(latent // 4, 2)
    features = enc.shape[0]
    ring_z = Ring(z, lambda q: (q * 2 + core, latent))
    ring_x = Ring(x, lambda q: (layer, q * 8 + zl * 4 + y))
    ring_y = Ring(y, lambda q: (layer, x * 8 + zl * 4 + q))
    core_peer = (z * 2 + 1 - core, latent)
    zl_peer = (layer, x * 8 + (1 - zl) * 4 + y)
    links = Links(send_sems, recv_sems, (layer, latent))

    dec_copy = pltpu.make_async_copy(dec_hbm, dec, local_sems.at[0])
    enc_copy = pltpu.make_async_copy(enc_hbm, enc, local_sems.at[1])
    bank_copy = pltpu.make_async_copy(bank_hbm, bank_ref, local_sems.at[5])
    small_copies = [
        pltpu.make_async_copy(src, dst, local_sems.at[6 + i])
        for i, (src, dst) in enumerate(((ids_hbm, ids_ref), (bias_hbm, bias_ref), (dbias_hbm, dbias_ref)))
    ]
    for copy in (bank_copy, *small_copies, dec_copy, enc_copy):
        copy.start()

    partners = [core_peer, zl_peer]
    for ring in (ring_x, ring_y, ring_z):
        partners += [ring.device(d) for d in (1, 2, 3)]
    barrier = pltpu.get_barrier_semaphore()
    for device in partners:
        pl.semaphore_signal(barrier, inc=1, device_id=device, device_id_type=MESH)
    pl.semaphore_wait(barrier, len(partners))

    def counts(rows):
        hits = (ids_ref[...][None, :] == rows).astype(F32)
        return jnp.sum(hits, axis=1, keepdims=True)

    def bank_rows(k, block, n):
        i = lax.broadcasted_iota(jnp.int32, (n, 1), 0)
        b = block + i // ROWS
        return ((b // 4 * 2 + k) * 4 + lax.rem(b, 4)) * ROWS + lax.rem(i, ROWS)

    def plane_first_start(tag, k, b0, b1):
        own = b0.at[k, x, y]
        direct_start(links, (tag + "0", k), ring_y, lambda q: own, lambda q: b0.at[k, x, q])
        own = b1.at[k, x, y]
        direct_start(links, (tag + "1", k), ring_x, lambda q: own, lambda q: b1.at[k, q, y])

    def plane_second_start(tag, k, b0, b1):
        links.recv((tag + "0", k), b0.at[k, x, pl.ds(0, 3)])
        own = b0.at[k, x]
        direct_start(links, (tag + "2", k), ring_x, lambda q: own, lambda q: b0.at[k, q])
        links.recv((tag + "1", k), b1.at[k, pl.ds(0, 3), y])
        block = b1.at[k, :, y]
        direct_start(links, (tag + "3", k), ring_y, lambda q: block, lambda q: b1.at[k, :, q])

    def plane_finish(tag, k, b0, b1):
        links.recv((tag + "2", k), b0.at[k, pl.ds(0, 3)])
        links.recv((tag + "3", k), b1.at[k, pl.ds(0, 3)])

    def z_part(s, k):
        return lambda q, h: sums.at[s, k, q, h]

    def z_got(s, k):
        return lambda i: zgot.at[s, k, i]

    def z_both(s, k):
        return lambda i: zboth.at[s, k, i]

    def z_view(buf, k):
        return lambda q, h: buf.at[k, core, q, h]

    def product_send(s, k):
        links.send(("core", s, k), parts.at[s, k, 1 - core], from_core.at[s, k], core_peer)

    def z_scatter_start(s, k):
        links.recv(("core", s, k), from_core.at[s, k])
        own = parts[s, k, core].astype(F32) + from_core[s, k].astype(F32)
        sums[s, k] = own.astype(BF)
        if Z_RS == "ring":
            scatter_start(links, ("zs", s, k), ring_z, z_part(s, k), z_got(s, k))
        else:
            direct_start(
                links,
                ("zs", s, k),
                ring_z,
                lambda q: sums.at[s, k, q],
                lambda q: zgot.at[s, k, pl.ds(2 * q, 2)],
            )

    def z_scatter_middle(s, k):
        if Z_RS == "ring":
            scatter_middle(links, ("zs", s, k), ring_z, z_part(s, k), z_got(s, k), z_both(s, k))

    def z_scatter_finish(s, k):
        if Z_RS == "ring":
            last_four = zgot.at[s, k, pl.ds(2, 4)]
            return scatter_finish(links, ("zs", s, k), ring_z, z_part(s, k), z_got(s, k), last_four)
        links.recv(("zs", s, k), zgot.at[s, k, pl.ds(0, 6)])
        total = sums[s, k, z].astype(F32)
        for shift in (1, 2, 3):
            total += zgot[s, k, pl.ds(2 * ring_z.at(shift), 2)].astype(F32)
        return total[0], total[1]

    def to_core(s, k, buf, shift):
        block = buf.at[k, core, ring_z.at(shift)]
        links.send(("zc", s, k), block, block, core_peer)

    def z_gather_start(s, k, buf):
        if Z_AG == "ring":
            gather_start(links, ("zg", s, k), ring_z, z_view(buf, k))
        else:
            own = buf.at[k, core, z]
            direct_start(links, ("zg", s, k), ring_z, lambda q: own, lambda q: buf.at[k, core, q])
        to_core(s, k, buf, 0)

    def z_gather_forward(s, k, buf):
        if Z_AG == "ring":
            gather_forward(links, ("zg", s, k), ring_z, z_view(buf, k))

    def z_gather_finish(s, k, buf):
        two = buf.at[k, core, 0]
        if Z_AG == "ring":
            links.recv(("zg", s, k, "own"), two)
            to_core(s, k, buf, -1)
            to_core(s, k, buf, 1)
            links.recv(("zg", s, k, "far"), two)
        else:
            links.recv(("zg", s, k), buf.at[k, core, pl.ds(0, 3)])
            to_core(s, k, buf, -1)
            to_core(s, k, buf, 1)
        to_core(s, k, buf, 2)
        links.recv(("zc", s, k), buf.at[k, 1 - core])

    def encode(k):
        b0 = bk0[k].reshape(256, F0)
        b1 = bk1[k].reshape(256, features - F0)

        def tile(n, carry):
            at = pl.ds(pl.multiple_of(n * 256, 256), 256)
            out = jnp.dot(b0, enc[:F0, at], preferred_element_type=F32)
            out += jnp.dot(b1, enc[F0:, at], preferred_element_type=F32)
            parts[0, k, :, :, :, :, at] = out.astype(BF).reshape(2, 4, 2, ROWS, 256)
            return carry

        lax.fori_loop(0, 4, tile, 0)
        product_send(0, k)

    def latents(k):
        halves = z_scatter_finish(0, k)
        for h in (0, 1):
            pre = halves[h] + bias_ref[...][None, :]
            soft = jnp.maximum(pre, 0.0) + jnp.log1p(jnp.exp(-jnp.abs(pre)))
            lat[k, core, z, h] = soft.astype(BF)
            slope[k, h] = jax.nn.sigmoid(pre)
        z_gather_start(0, k, lat)

    def decode(k):
        rows = lat[k].reshape(256, -1)
        over = (((1,), (1,)), ((), ()))
        out = lax.dot_general(rows, dec[:F0], over, preferred_element_type=F32)
        rp0[k] = out.astype(BF).reshape(4, 4, ROWS, F0)
        direct_start(links, ("xs", k), ring_x, lambda q: rp0.at[k, q], lambda q: got0.at[k, q])
        out = lax.dot_general(rows, dec[F0:], over, preferred_element_type=F32)
        rp1[k] = out.astype(BF).reshape(4, 4, ROWS, features - F0)
        direct_start(links, ("ys", k), ring_y, lambda q: rp1.at[k, :, q], lambda q: got1.at[k, q])

    def recon_second(k):
        links.recv(("xs", k), got0.at[k, pl.ds(0, 3)])
        total = rp0[k, x].astype(F32)
        for shift in (1, 2, 3):
            total += got0[k, ring_x.at(shift)].astype(F32)
        s0[k] = total.astype(BF)
        direct_start(links, ("xt", k), ring_y, lambda q: s0.at[k, q], lambda q: d0.at[k, q])
        links.recv(("ys", k), got1.at[k, pl.ds(0, 3)])
        total = rp1[k, :, y].astype(F32)
        for shift in (1, 2, 3):
            total += got1[k, ring_y.at(shift)].astype(F32)
        s1[k] = total.astype(BF)
        direct_start(links, ("yt", k), ring_x, lambda q: s1.at[k, q], lambda q: d1.at[k, q])

    def recon_third(k):
        for tag, ring, s, d, q, e in (("xt", ring_y, s0, d0, q0, e0), ("yt", ring_x, s1, d1, q1, e1)):
            links.recv((tag, k), d.at[k, pl.ds(0, 3)])
            total = s[k, ring.at(0)].astype(F32)
            for shift in (1, 2, 3):
                total += d[k, ring.at(shift)].astype(F32)
            q[k] = total.astype(BF)
            links.send((tag + "z", k), q.at[k], e.at[k], zl_peer)

    def residual(k):
        own_counts = counts(bank_rows(k, x * 4 + y, ROWS))
        for tag, at, q, e, bk, rs in (
            ("xt", pl.ds(0, F0), q0, e0, bk0, rs0),
            ("yt", pl.ds(F0, features - F0), q1, e1, bk1, rs1),
        ):
            links.recv((tag + "z", k), e.at[k])
            recon = q[k].astype(F32) + e[k].astype(F32) + dbias_ref[at][None, :]
            value = (recon - bk[k, x, y].astype(F32)) * scale
            rs[k, x, y] = (value * own_counts).astype(BF)
        plane_first_start("r", k, rs0, rs1)

    def backward(k):
        r0 = rs0[k].reshape(256, F0)
        r1 = rs1[k].reshape(256, features - F0)

        def tile(n, carry):
            at = pl.ds(pl.multiple_of(n * 256, 256), 256)
            out = jnp.dot(r0, dec[:F0, at], preferred_element_type=F32)
            out += jnp.dot(r1, dec[F0:, at], preferred_element_type=F32)
            parts[1, k, :, :, :, :, at] = out.astype(BF).reshape(2, 4, 2, ROWS, 256)
            return carry

        lax.fori_loop(0, 4, tile, 0)
        product_send(1, k)

    def latent_gradient(k):
        row_counts = counts(bank_rows(k, core * 8 + z * 2, 2 * ROWS))
        total_norm = norms_ref[0:1] + norms_ref[1:2] + norms_ref[2:3]
        halves = z_scatter_finish(1, k)
        for h in (0, 1):
            weight = row_counts[h * ROWS : (h + 1) * ROWS]
            grad = halves[h] + weight * (PENALTY * scale * total_norm)
            pg[k, core, z, h] = (grad * slope[k, h]).astype(BF)
        z_gather_start(1, k, pg)

    def bank_send():
        bank_copy.wait()
        blk0[zl] = bank_ref[:, :F0]
        blk1[zl] = bank_ref[:, F0:]
        links.send(("bz0",), blk0.at[zl], blk0.at[zl], zl_peer)
        links.send(("bz1",), blk1.at[zl], blk1.at[zl], zl_peer)

    def bank_recv():
        links.recv(("bz0",), blk0.at[1 - zl])
        links.recv(("bz1",), blk1.at[1 - zl])
        for k in range(CHUNKS):
            bk0[k, x, y] = blk0[k]
            bk1[k, x, y] = blk1[k]
            plane_first_start("b", k, bk0, bk1)

    def squares_send():
        for copy in (*small_copies, dec_copy):
            copy.wait()
        row = lax.broadcasted_iota(jnp.int32, (8, features), 0)
        column = lax.broadcasted_iota(jnp.int32, (8, features), 1) + layer * features
        owner = jnp.where((column >= row * D) & (column < (row + 1) * D), 1.0, 0.0).astype(BF)

        def square(n, carry):
            at = pl.ds(pl.multiple_of(n * 256, 256), 256)
            wide = dec[:, at].astype(F32)
            wide = wide * wide
            high = wide.astype(BF)
            low = (wide - high.astype(F32)).astype(BF)
            total = jnp.dot(owner, high, preferred_element_type=F32)
            total += jnp.dot(owner, low, preferred_element_type=F32)
            sq_part[:, at] = total
            return carry

        lax.fori_loop(0, 4, square, 0)
        links.send(("sqc",), sq_part, sq_core, core_peer)

    def squares_second():
        links.recv(("sqc",), sq_core)
        sq_chip[...] = sq_part[...] + sq_core[...]
        direct_start(links, ("sqz",), ring_z, lambda q: sq_chip, lambda q: sq_z.at[q])

    def squares_sum():
        links.recv(("sqz",), sq_z.at[pl.ds(0, 3)])
        squares = sq_chip[...]
        for shift in (1, 2, 3):
            squares += sq_z[ring_z.at(shift)]
        norms_ref[...] = jnp.sqrt(squares + 1e-6)

    def copy_out(i, src, dst):
        copy = pltpu.make_async_copy(src, dst, local_sems.at[i])
        copy.start()
        outgoing.append(copy)

    def coefficients():
        colsum = jnp.zeros((1, lat.shape[-1]), F32)
        for k in range(CHUNKS):
            weight = counts(bank_rows(k, 0, 256))
            colsum += jnp.sum(lat[k].reshape(256, -1).astype(F32) * weight, axis=0, keepdims=True)
        coef_ref[...] = (PENALTY * scale * colsum) / norms_ref[...]

    def turn(buf, k, pair):
        at = pl.ds(256 * k, 256)
        buf[:F0, at] = pair[0][k].reshape(256, F0).T
        buf[F0:, at] = pair[1][k].reshape(256, features - F0).T

    def decoder_gradient(first, last):
        feature = layer * features + lax.broadcasted_iota(jnp.int32, (features, 1), 0)

        def tile(n, carry):
            at = pl.ds(pl.multiple_of(n * 256, 256), 256)
            out = jnp.zeros((features, 256), F32)
            for k in range(CHUNKS):
                rows = lat[k, :, :, :, :, at].reshape(256, 256)
                out += jnp.dot(resid_turned[:, 256 * k : 256 * k + 256], rows, preferred_element_type=F32)
            spread = jnp.where(
                feature < D, coef_ref[0:1, at], jnp.where(feature < 2 * D, coef_ref[1:2, at], coef_ref[2:3, at])
            )
            dgrad[:, at] = (out + spread * dec[:, at].astype(F32)).astype(BF)
            return carry

        lax.fori_loop(first, last, tile, 0)

    outgoing = []
    bank, resid = (bk0, bk1), (rs0, rs1)
    steps = [
        (bank_send,),
        (bank_recv,),
        (squares_send,),
        (plane_second_start, "b", 0, *bank),
        (squares_second,),
        (plane_second_start, "b", 1, *bank),
        (enc_copy.wait,),
        (plane_finish, "b", 0, *bank),
        (encode, 0),
        (z_scatter_start, 0, 0),
        (plane_finish, "b", 1, *bank),
        (encode, 1),
        (z_scatter_middle, 0, 0),
        (z_scatter_start, 0, 1),
        (turn, turned, 0, bank),
        (turn, turned, 1, bank),
        (copy_out, 2, turned, turned_out),
        (squares_sum,),
        (latents, 0),
        (z_scatter_middle, 0, 1),
        (z_gather_forward, 0, 0, lat),
        (latents, 1),
        (z_gather_finish, 0, 0, lat),
        (decode, 0),
        (z_gather_forward, 0, 1, lat),
        (z_gather_finish, 0, 1, lat),
        (decode, 1),
        (coefficients,),
        (recon_second, 0),
        (recon_third, 0),
        (recon_second, 1),
        (residual, 0),
        (recon_third, 1),
        (plane_second_start, "r", 0, *resid),
        (residual, 1),
        (plane_second_start, "r", 1, *resid),
        (plane_finish, "r", 0, *resid),
        (backward, 0),
        (z_scatter_start, 1, 0),
        (turn, resid_turned, 0, resid),
        (plane_finish, "r", 1, *resid),
        (backward, 1),
        (z_scatter_middle, 1, 0),
        (z_scatter_start, 1, 1),
        (turn, resid_turned, 1, resid),
        (decoder_gradient, 0, 2),
        (latent_gradient, 0),
        (z_scatter_middle, 1, 1),
        (z_gather_forward, 1, 0, pg),
        (latent_gradient, 1),
        (decoder_gradient, 2, 4),
        (copy_out, 3, dgrad, dgrad_out),
        (z_gather_finish, 1, 0, pg),
        (z_gather_forward, 1, 1, pg),
        (z_gather_finish, 1, 1, pg),
        (copy_out, 4, pg, pg_out),
    ]
    for step, *given in steps:
        step(*given)
    for family, view in (
        ("bz0", blk0.at[0]),
        ("bz1", blk1.at[0]),
        ("b0", s0.at[:, pl.ds(0, 3)]),
        ("b1", s1.at[:, pl.ds(0, 3)]),
        ("b2", got0.at[:, pl.ds(0, 3)]),
        ("b3", got1.at[:, pl.ds(0, 3)]),
        ("sqc", sq_part),
        ("sqz", sq_z.at[pl.ds(0, 3)]),
        ("core", sums),
        ("zs", zgot.at[:, :, pl.ds(0, 6)]),
        ("zg", zgot.at[:, :, pl.ds(0, 6)]),
        ("zc", sums),
        ("xs", got0.at[:, pl.ds(0, 3)]),
        ("ys", got1.at[:, pl.ds(0, 3)]),
        ("xt", s0.at[:, pl.ds(0, 3)]),
        ("yt", s1.at[:, pl.ds(0, 3)]),
        ("xtz", q0),
        ("ytz", q1),
        ("r0", s0.at[:, pl.ds(0, 3)]),
        ("r1", s1.at[:, pl.ds(0, 3)]),
        ("r2", got0.at[:, pl.ds(0, 3)]),
        ("r3", got1.at[:, pl.ds(0, 3)]),
    ):
        links.sent(family, view)
    for copy in outgoing:
        copy.wait()


def shards(ids, bank, enc_weight, enc_bias, dec_weight, dec_bias):
    tokens = ids.shape[0]
    features, lats = enc_weight.shape
    dec = dec_weight.T
    f1 = features - F0
    scale = 1.0 / math.sqrt(tokens)
    k = CHUNKS
    operands = (ids, bank, enc_bias, dec_bias, enc_weight, dec)
    messages = 68
    turned, dgrad, pg = pl.pallas_call(
        functools.partial(kernel, scale),
        out_shape=[
            jax.ShapeDtypeStruct((features, k * 256), BF),
            jax.ShapeDtypeStruct((features, lats), BF),
            jax.ShapeDtypeStruct((k, 2, 4, 2, ROWS, lats), BF),
        ],
        in_specs=[pl.BlockSpec(memory_space=pl.ANY)] * 6,
        out_specs=[pl.BlockSpec(memory_space=pl.ANY)] * 3,
        scratch_shapes=[
            pltpu.VMEM(ids.shape, jnp.int32),
            pltpu.VMEM(bank.shape, BF),
            pltpu.VMEM(enc_bias.shape, F32),
            pltpu.VMEM(dec_bias.shape, F32),
            pltpu.VMEM((features, lats), BF),
            pltpu.VMEM((features, lats), BF),
            pltpu.VMEM((2, ROWS, F0), BF),
            pltpu.VMEM((2, ROWS, f1), BF),
            pltpu.VMEM((k, 4, 4, ROWS, F0), BF),
            pltpu.VMEM((k, 4, 4, ROWS, f1), BF),
            pltpu.VMEM((2, k, 2, 4, 2, ROWS, lats), BF),
            pltpu.VMEM((2, k, 4, 2, ROWS, lats), BF),
            pltpu.VMEM((2, k, 4, 2, ROWS, lats), BF),
            pltpu.VMEM((2, k, 8, ROWS, lats), BF),
            pltpu.VMEM((2, k, 2, ROWS, lats), BF),
            pltpu.VMEM((k, 2, 4, 2, ROWS, lats), BF),
            pltpu.VMEM((k, 2, 4, 2, ROWS, lats), BF),
            pltpu.VMEM((k, 2, ROWS, lats), F32),
            pltpu.VMEM((k, 4, 4, ROWS, F0), BF),
            pltpu.VMEM((k, 4, 4, ROWS, f1), BF),
            pltpu.VMEM((k, 4, 4, ROWS, F0), BF),
            pltpu.VMEM((k, 4, 4, ROWS, f1), BF),
            pltpu.VMEM((k, 4, ROWS, F0), BF),
            pltpu.VMEM((k, 4, ROWS, f1), BF),
            pltpu.VMEM((k, 4, ROWS, F0), BF),
            pltpu.VMEM((k, 4, ROWS, f1), BF),
            pltpu.VMEM((k, ROWS, F0), BF),
            pltpu.VMEM((k, ROWS, f1), BF),
            pltpu.VMEM((k, ROWS, F0), BF),
            pltpu.VMEM((k, ROWS, f1), BF),
            pltpu.VMEM((k, 4, 4, ROWS, F0), BF),
            pltpu.VMEM((k, 4, 4, ROWS, f1), BF),
            pltpu.VMEM((8, lats), F32),
            pltpu.VMEM((8, lats), F32),
            pltpu.VMEM((8, lats), F32),
            pltpu.VMEM((4, 8, lats), F32),
            pltpu.VMEM((8, lats), F32),
            pltpu.VMEM((8, lats), F32),
            pltpu.VMEM((features, k * 256), BF),
            pltpu.VMEM((features, k * 256), BF),
            pltpu.VMEM((features, lats), BF),
            pltpu.SemaphoreType.DMA((22,)),
            pltpu.SemaphoreType.DMA((messages,)),
            pltpu.SemaphoreType.DMA((9,)),
        ],
        compiler_params=pltpu.CompilerParams(
            collective_id=0, has_side_effects=True, vmem_limit_bytes=40 * 2**20
        ),
        name="crosscoder_step",
    )(*(pltpu.with_memory_space_constraint(a, pltpu.HBM) for a in operands))

    grad_encoder, grad_decoder = gradients(turned, pg.reshape(-1, lats), dgrad)
    return grad_encoder, grad_decoder.T


def gradients_kernel(turned, pg, dgrad, enc_grad, dec_grad):
    dec_grad[...] = dgrad[...]
    enc_grad[...] = jnp.dot(turned[...], pg[...], preferred_element_type=F32).astype(BF)


def gradients(turned, pg, dgrad):
    features, lats = dgrad.shape
    size = features // 3
    piece = lambda a: pl.BlockSpec((size, a.shape[1]), lambda n: (n, 0))
    whole = pl.BlockSpec(pg.shape, lambda n: (0, 0))
    return pl.pallas_call(
        gradients_kernel,
        out_shape=[jax.ShapeDtypeStruct(dgrad.shape, BF)] * 2,
        grid=(3,),
        in_specs=[piece(turned), whole, piece(dgrad)],
        out_specs=[piece(dgrad), piece(dgrad)],
        compiler_params=pltpu.CompilerParams(vmem_limit_bytes=24 * 2**20),
        name="gradients",
    )(turned, pg, dgrad)


def solution(mesh):
    in_specs = (
        P(),
        P("latent", "layer"),
        P("layer", "latent"),
        P("latent"),
        P("latent", "layer"),
        P("layer"),
    )
    out_specs = (P("layer", "latent"), P("latent", "layer"))
    return jax.shard_map(shards, mesh=mesh, in_specs=in_specs, out_specs=out_specs, check_vma=False)
```

```python
import functools
import math

import jax
import jax.numpy as jnp
from jax import lax
from jax.experimental import pallas as pl
from jax.experimental.pallas import tpu as pltpu
from jax.sharding import PartitionSpec as P

D = 3584
LAYERS = 3
PENALTY = 0.3
ROWS = 16
F0 = 640
CHUNKS = 4
LAG = 4.5
MESH = pl.DeviceIdType.MESH
BF = jnp.bfloat16
F32 = jnp.float32


class Links:
    def __init__(self, send_sems, recv_sems, me):
        self.send_sems, self.recv_sems, self.me = send_sems, recv_sems, me
        self.names, self.families = {}, {}

    def copy(self, name, src, dst, device):
        i = self.names.setdefault(name, len(self.names))
        j = self.families.setdefault(name[0], len(self.families))
        return pltpu.make_async_remote_copy(
            src_ref=src,
            dst_ref=dst,
            send_sem=self.send_sems.at[j],
            recv_sem=self.recv_sems.at[i],
            device_id=device,
            device_id_type=MESH,
        )

    def send(self, name, src, dst, device):
        self.copy(name, src, dst, device).start()

    def recv(self, name, view):
        self.copy(name, view, view, self.me).wait_recv()

    def sent(self, family, view):
        i = self.families[family]
        pltpu.make_async_copy(view, view, self.send_sems.at[i]).wait()


class Ring:
    def __init__(self, place, device_at):
        self.place, self.device_at = place, device_at

    def at(self, shift):
        return lax.rem(self.place + shift % 4, 4)

    def device(self, shift):
        return self.device_at(self.at(shift))


def direct_start(links, tag, ring, source, target):
    for d in (2, 1, 3):
        links.send(tag, source(ring.at(d)), target(ring.at(0)), ring.device(d))


def kernel(
    scale,
    ids_hbm, bank_hbm, bias_hbm, dbias_hbm, enc_hbm, dec_hbm,
    turned_out, dgrad_out, pg_out,
    ids_ref, bank_ref, bias_ref, dbias_ref, enc, dec, blk0, blk1, bk0, bk1,
    parts, from_core, sums, zgot, lat, pg, slope,
    rp0, rp1, got0, got1, s0, s1, d0, d1, q0, q1, e0, e1, rs0, rs1,
    sq_part, sq_core, sq_chip, sq_z, norms_ref, coef_ref, turned, resid_turned, dgrad,
    send_sems, recv_sems, local_sems,
):
    layer, latent = lax.axis_index("layer"), lax.axis_index("latent")
    z, core = layer // 2, lax.rem(layer, 2)
    x, y = latent // 8, lax.rem(latent, 4)
    zl = lax.rem(latent // 4, 2)
    features = enc.shape[0]
    ring_z = Ring(z, lambda q: (q * 2 + core, latent))
    ring_x = Ring(x, lambda q: (layer, q * 8 + zl * 4 + y))
    ring_y = Ring(y, lambda q: (layer, x * 8 + zl * 4 + q))
    core_peer = (z * 2 + 1 - core, latent)
    zl_peer = (layer, x * 8 + (1 - zl) * 4 + y)
    links = Links(send_sems, recv_sems, (layer, latent))

    dec_copy = pltpu.make_async_copy(dec_hbm, dec, local_sems.at[0])
    enc_copy = pltpu.make_async_copy(enc_hbm, enc, local_sems.at[1])
    bank_copy = pltpu.make_async_copy(bank_hbm, bank_ref, local_sems.at[5])
    small_copies = [
        pltpu.make_async_copy(src, dst, local_sems.at[6 + i])
        for i, (src, dst) in enumerate(((ids_hbm, ids_ref), (bias_hbm, bias_ref), (dbias_hbm, dbias_ref)))
    ]
    for copy in (bank_copy, *small_copies, dec_copy, enc_copy):
        copy.start()

    partners = [core_peer, zl_peer]
    for ring in (ring_x, ring_y, ring_z):
        partners += [ring.device(d) for d in (1, 2, 3)]
    barrier = pltpu.get_barrier_semaphore()
    for device in partners:
        pl.semaphore_signal(barrier, inc=1, device_id=device, device_id_type=MESH)
    pl.semaphore_wait(barrier, len(partners))

    def counts(rows):
        hits = (ids_ref[...][None, :] == rows).astype(F32)
        return jnp.sum(hits, axis=1, keepdims=True)

    def bank_rows(k, block, n, stride=1):
        i = lax.broadcasted_iota(jnp.int32, (n, 1), 0)
        j = block + stride * (i // ROWS)
        at_x = j // 2
        at_y = 2 * lax.rem(j, 2) + lax.rem(at_x + k % 2, 2)
        return ((at_x * 2 + k // 2) * 4 + at_y) * ROWS + lax.rem(i, ROWS)

    def first(buf, k, q):
        return buf.at[k, q]

    def other(buf, k, q):
        return buf.at[k, :, lax.rem(q + k % 2, 2), q // 2]

    def bank_first(k, q):
        return bk0.at[k // 2, q, :, lax.rem(q + k % 2, 2)]

    def bank_other(k, q):
        return bk1.at[k // 2, :, lax.rem(q + k % 2, 2), q]

    def bank_spread(k):
        direct_start(links, ("b2", k), ring_x, lambda q: bank_first(k, x), lambda q: bank_first(k, q))
        direct_start(links, ("b3", k), ring_y, lambda q: bank_other(k, y), lambda q: bank_other(k, q))

    def bank_chunk(k):
        low, odd = k // 2, k % 2
        places = [(i, 2 * j + (i + odd) % 2) for i in range(4) for j in range(2)]
        b0 = [bk0[low, i, j // 2, j % 2] for i, j in places]
        b1 = [bk1[low, i // 2, i % 2, j] for i, j in places]
        return jnp.concatenate(b0, axis=0), jnp.concatenate(b1, axis=0)

    def product(s, k, left, weight):
        def tile(n, carry):
            at = pl.ds(pl.multiple_of(n * 256, 256), 256)
            out = jnp.dot(left[0], weight[:F0, at], preferred_element_type=F32)
            out += jnp.dot(left[1], weight[F0:, at], preferred_element_type=F32)
            parts[s, k, :, :, :, at] = out.astype(BF).reshape(2, 4, ROWS, 256)
            return carry

        lax.fori_loop(0, 4, tile, 0)
        links.send(("core", s, k), parts.at[s, k, 1 - core], from_core.at[s, k], core_peer)

    def z_scatter(s, k):
        links.recv(("core", s, k), from_core.at[s, k])
        own = parts[s, k, core].astype(F32) + from_core[s, k].astype(F32)
        sums[s, k] = own.astype(BF)
        direct_start(
            links, ("zs", s, k), ring_z, lambda q: sums.at[s, k, q], lambda q: zgot.at[s, k, q]
        )

    def z_sum(s, k):
        links.recv(("zs", s, k), zgot.at[s, k, pl.ds(0, 3)])
        total = sums[s, k, z].astype(F32)
        for shift in (1, 2, 3):
            total += zgot[s, k, ring_z.at(shift)].astype(F32)
        return total

    def to_core(s, k, buf, shift):
        block = buf.at[k, core, ring_z.at(shift)]
        links.send(("zc", s, k), block, block, core_peer)

    def z_gather(s, k, buf):
        own = buf.at[k, core, z]
        direct_start(links, ("zg", s, k), ring_z, lambda q: own, lambda q: buf.at[k, core, q])
        to_core(s, k, buf, 0)

    def z_pass(s, k, buf):
        links.recv(("zg", s, k), buf.at[k, core, pl.ds(0, 3)])
        for shift in (1, 2, 3):
            to_core(s, k, buf, shift)

    def z_finish(s, k, buf):
        links.recv(("zc", s, k), buf.at[k, 1 - core])

    def encode(k):
        links.recv(("b2", k), got0.at[k, pl.ds(0, 3)])
        links.recv(("b3", k), got1.at[k, pl.ds(0, 3)])
        product(0, k, bank_chunk(k), enc)

    def latents(k):
        pre = z_sum(0, k) + bias_ref[...][None, :]
        soft = jnp.maximum(pre, 0.0) + jnp.log1p(jnp.exp(-jnp.abs(pre)))
        lat[k, core, z] = soft.astype(BF)
        slope[k] = jax.nn.sigmoid(pre)
        z_gather(0, k, lat)

    def decode(k):
        z_finish(0, k, lat)
        rows = lat[k].reshape(128, -1)
        over = (((1,), (1,)), ((), ()))
        out = lax.dot_general(rows, dec[:F0], over, preferred_element_type=F32)
        rp0[k] = out.astype(BF).reshape(4, 2, ROWS, F0)
        direct_start(links, ("xs", k), ring_x, lambda q: first(rp0, k, q), lambda q: got0.at[k, q])
        out = lax.dot_general(rows, dec[F0:], over, preferred_element_type=F32)
        rp1[k] = out.astype(BF).reshape(2, 2, 2, ROWS, features - F0)
        direct_start(links, ("ys", k), ring_y, lambda q: other(rp1, k, q), lambda q: got1.at[k, q])

    def recon_second(k):
        for tag, ring, own, got, s, d, next_ring in (
            ("x", ring_x, first(rp0, k, x), got0, s0, d0, ring_y),
            ("y", ring_y, other(rp1, k, y), got1, s1, d1, ring_x),
        ):
            links.recv((tag + "s", k), got.at[k, pl.ds(0, 3)])
            total = own[...].astype(F32)
            for shift in (1, 2, 3):
                total += got[k, ring.at(shift)].astype(F32)
            s[k] = total.astype(BF)
            direct_start(links, (tag + "t", k), next_ring, lambda q: s.at[k], lambda q: d.at[k, q])

    def recon_third(k):
        for tag, ring, s, d, t, e in (("xt", ring_y, s0, d0, q0, e0), ("yt", ring_x, s1, d1, q1, e1)):
            links.recv((tag, k), d.at[k, pl.ds(0, 3)])
            total = s[k].astype(F32)
            for shift in (1, 2, 3):
                total += d[k, ring.at(shift)].astype(F32)
            t[k] = total.astype(BF)
            links.send((tag + "z", k), t.at[k], e.at[k], zl_peer)

    def residual(k):
        j = 2 * lax.rem(y + k % 2, 2) + y // 2
        for tag, at, t, e, inputs, out, rows in (
            ("xt", pl.ds(0, F0), q0, e0, bank_first(k, x), first(rs0, k, x), bank_rows(k, 2 * x, 32)),
            ("yt", pl.ds(F0, features - F0), q1, e1, bank_other(k, y), other(rs1, k, y), bank_rows(k, j, 32, 4)),
        ):
            links.recv((tag + "z", k), e.at[k])
            weight = counts(rows) * scale
            for b in (0, 1):
                recon = t[k, b].astype(F32) + e[k, b].astype(F32) + dbias_ref[at][None, :]
                value = recon - inputs[b].astype(F32)
                out[b] = (value * weight[b * ROWS : (b + 1) * ROWS]).astype(BF)
        direct_start(links, ("r2", k), ring_x, lambda q: first(rs0, k, x), lambda q: first(rs0, k, q))
        direct_start(links, ("r3", k), ring_y, lambda q: other(rs1, k, y), lambda q: other(rs1, k, q))

    def resid_chunk(k):
        return rs0[k].reshape(128, F0), rs1[k].reshape(128, features - F0)

    def backward(k):
        links.recv(("r2", k), got0.at[k, pl.ds(0, 3)])
        links.recv(("r3", k), got1.at[k, pl.ds(0, 3)])
        product(1, k, resid_chunk(k), dec)

    def latent_gradient(k):
        weight = counts(bank_rows(k, core * 4 + z, ROWS))
        total_norm = norms_ref[0:1] + norms_ref[1:2] + norms_ref[2:3]
        grad = z_sum(1, k) + weight * (PENALTY * scale * total_norm)
        pg[k, core, z] = (grad * slope[k]).astype(BF)
        z_gather(1, k, pg)

    def bank_send():
        bank_copy.wait()
        blk0[zl] = bank_ref[:, :F0]
        blk1[zl] = bank_ref[:, F0:]
        links.send(("bz0",), blk0.at[zl], blk0.at[zl], zl_peer)
        links.send(("bz1",), blk1.at[zl], blk1.at[zl], zl_peer)

    def bank_recv():
        links.recv(("bz0",), blk0.at[1 - zl])
        links.recv(("bz1",), blk1.at[1 - zl])
        for low in (0, 1):
            own0 = bk0.at[low, x, y // 2, lax.rem(y, 2)]
            own1 = bk1.at[low, x // 2, lax.rem(x, 2), y]
            own0[...] = blk0[low]
            own1[...] = blk1[low]
            direct_start(
                links, ("b0", low), ring_y, lambda q: own0, lambda q: bk0.at[low, x, q // 2, lax.rem(q, 2)]
            )
            direct_start(
                links, ("b1", low), ring_x, lambda q: own1, lambda q: bk1.at[low, q // 2, lax.rem(q, 2), y]
            )

    def bank_second(low):
        links.recv(("b0", low), e0.at[pl.ds(0, 3), 0])
        links.recv(("b1", low), e1.at[pl.ds(0, 3), 0])
        bank_spread(2 * low)
        bank_spread(2 * low + 1)

    def squares_send():
        for copy in (*small_copies, dec_copy):
            copy.wait()
        row = lax.broadcasted_iota(jnp.int32, (8, features), 0)
        column = lax.broadcasted_iota(jnp.int32, (8, features), 1) + layer * features
        owner = jnp.where((column >= row * D) & (column < (row + 1) * D), 1.0, 0.0).astype(BF)

        def square(n, carry):
            at = pl.ds(pl.multiple_of(n * 256, 256), 256)
            wide = dec[:, at].astype(F32)
            wide = wide * wide
            high = wide.astype(BF)
            low = (wide - high.astype(F32)).astype(BF)
            total = jnp.dot(owner, high, preferred_element_type=F32)
            total += jnp.dot(owner, low, preferred_element_type=F32)
            sq_part[:, at] = total
            return carry

        lax.fori_loop(0, 4, square, 0)
        links.send(("sqc",), sq_part, sq_core, core_peer)

    def squares_second():
        links.recv(("sqc",), sq_core)
        sq_chip[...] = sq_part[...] + sq_core[...]
        direct_start(links, ("sqz",), ring_z, lambda q: sq_chip, lambda q: sq_z.at[q])

    def squares_sum():
        links.recv(("sqz",), sq_z.at[pl.ds(0, 3)])
        squares = sq_chip[...]
        for shift in (1, 2, 3):
            squares += sq_z[ring_z.at(shift)]
        norms_ref[...] = jnp.sqrt(squares + 1e-6)

    def copy_out(i, src, dst):
        copy = pltpu.make_async_copy(src, dst, local_sems.at[i])
        copy.start()
        outgoing.append(copy)

    def coefficients():
        colsum = jnp.zeros((1, lat.shape[-1]), F32)
        for k in range(CHUNKS):
            weight = counts(bank_rows(k, 0, 128))
            colsum += jnp.sum(lat[k].reshape(128, -1).astype(F32) * weight, axis=0, keepdims=True)
        coef_ref[...] = (PENALTY * scale * colsum) / norms_ref[...]

    def turn(buf, chunk, k):
        at = pl.ds(128 * k, 128)
        b0, b1 = chunk(k)
        buf[:F0, at] = b0.T
        buf[F0:, at] = b1.T

    def decoder_gradient(first, last):
        feature = layer * features + lax.broadcasted_iota(jnp.int32, (features, 1), 0)

        def tile(n, carry):
            at = pl.ds(pl.multiple_of(n * 256, 256), 256)
            rows = lat[:, :, :, :, at].reshape(512, 256)
            out = jnp.dot(resid_turned[...], rows, preferred_element_type=F32)
            spread = jnp.where(
                feature < D, coef_ref[0:1, at], jnp.where(feature < 2 * D, coef_ref[1:2, at], coef_ref[2:3, at])
            )
            dgrad[:, at] = (out + spread * dec[:, at].astype(F32)).astype(BF)
            return carry

        lax.fori_loop(first, last, tile, 0)

    outgoing = []
    chunk_steps = (
        (0.0, encode),
        (1.8, lambda k: z_scatter(0, k)),
        (8.0, latents),
        (14.3, lambda k: z_pass(0, k, lat)),
        (15.5, decode),
        (20.5, recon_second),
        (25.5, recon_third),
        (30.0, residual),
        (35.0, backward),
        (37.0, lambda k: z_scatter(1, k)),
        (43.0, latent_gradient),
        (49.5, lambda k: z_pass(1, k, pg)),
        (50.5, lambda k: z_finish(1, k, pg)),
    )
    once = (
        (-8.0, bank_send),
        (-7.0, bank_recv),
        (-6.0, squares_send),
        (-5.0, lambda: bank_second(0)),
        (-4.0, squares_second),
        (-3.0, lambda: bank_second(1)),
        (-2.0, enc_copy.wait),
        (9.0, squares_sum),
        (3 * LAG + 1.7, lambda: turn(turned, bank_chunk, 0)),
        (3 * LAG + 1.71, lambda: turn(turned, bank_chunk, 1)),
        (3 * LAG + 1.72, lambda: turn(turned, bank_chunk, 2)),
        (3 * LAG + 1.73, lambda: turn(turned, bank_chunk, 3)),
        (3 * LAG + 1.74, lambda: copy_out(2, turned, turned_out)),
        (3 * LAG + 16.0, coefficients),
        (3 * LAG + 36.5, lambda: turn(resid_turned, resid_chunk, 0)),
        (3 * LAG + 36.6, lambda: turn(resid_turned, resid_chunk, 1)),
        (3 * LAG + 37.1, lambda: turn(resid_turned, resid_chunk, 2)),
        (3 * LAG + 37.2, lambda: turn(resid_turned, resid_chunk, 3)),
        (3 * LAG + 37.3, lambda: decoder_gradient(0, 2)),
        (3 * LAG + 43.1, lambda: decoder_gradient(2, 4)),
        (3 * LAG + 43.2, lambda: copy_out(3, dgrad, dgrad_out)),
        (3 * LAG + 51.0, lambda: copy_out(4, pg, pg_out)),
    )
    timed = [(at, step, ()) for at, step in once]
    for k in range(CHUNKS):
        timed += [(at + LAG * k, step, (k,)) for at, step in chunk_steps]
    steps = [(step, *given) for at, step, given in sorted(timed, key=lambda entry: entry[0])]
    for step, *given in steps:
        step(*given)
    for family, view in (
        ("bz0", blk0.at[0]),
        ("bz1", blk1.at[0]),
        ("b0", e0.at[pl.ds(0, 3)]),
        ("b1", e1.at[pl.ds(0, 3)]),
        ("b2", got0.at[:, pl.ds(0, 3)]),
        ("b3", got1.at[:, pl.ds(0, 3)]),
        ("sqc", sq_part),
        ("sqz", sq_z.at[pl.ds(0, 3)]),
        ("core", sums),
        ("zs", zgot.at[:, :, pl.ds(0, 3)]),
        ("zg", zgot.at[:, :, pl.ds(0, 3)]),
        ("zc", sums),
        ("xs", got0.at[:, pl.ds(0, 3)]),
        ("ys", got1.at[:, pl.ds(0, 3)]),
        ("xt", got0.at[:, pl.ds(0, 3)]),
        ("yt", got1.at[:, pl.ds(0, 3)]),
        ("xtz", e0),
        ("ytz", e1),
        ("r2", got0.at[:, pl.ds(0, 3)]),
        ("r3", got1.at[:, pl.ds(0, 3)]),
    ):
        links.sent(family, view)
    for copy in outgoing:
        copy.wait()


def shards(ids, bank, enc_weight, enc_bias, dec_weight, dec_bias):
    tokens = ids.shape[0]
    features, lats = enc_weight.shape
    dec = dec_weight.T
    f1 = features - F0
    scale = 1.0 / math.sqrt(tokens)
    k = CHUNKS
    operands = (ids, bank, enc_bias, dec_bias, enc_weight, dec)
    messages = 80
    turned, dgrad, pg = pl.pallas_call(
        functools.partial(kernel, scale),
        out_shape=[
            jax.ShapeDtypeStruct((features, k * 128), BF),
            jax.ShapeDtypeStruct((features, lats), BF),
            jax.ShapeDtypeStruct((k, 2, 4, ROWS, lats), BF),
        ],
        in_specs=[pl.BlockSpec(memory_space=pl.ANY)] * 6,
        out_specs=[pl.BlockSpec(memory_space=pl.ANY)] * 3,
        scratch_shapes=[
            pltpu.VMEM(ids.shape, jnp.int32),
            pltpu.VMEM(bank.shape, BF),
            pltpu.VMEM(enc_bias.shape, F32),
            pltpu.VMEM(dec_bias.shape, F32),
            pltpu.VMEM((features, lats), BF),
            pltpu.VMEM((features, lats), BF),
            pltpu.VMEM((2, ROWS, F0), BF),
            pltpu.VMEM((2, ROWS, f1), BF),
            pltpu.VMEM((2, 4, 2, 2, ROWS, F0), BF),
            pltpu.VMEM((2, 2, 2, 4, ROWS, f1), BF),
            pltpu.VMEM((2, k, 2, 4, ROWS, lats), BF),
            pltpu.VMEM((2, k, 4, ROWS, lats), BF),
            pltpu.VMEM((2, k, 4, ROWS, lats), BF),
            pltpu.VMEM((2, k, 4, ROWS, lats), BF),
            pltpu.VMEM((k, 2, 4, ROWS, lats), BF),
            pltpu.VMEM((k, 2, 4, ROWS, lats), BF),
            pltpu.VMEM((k, ROWS, lats), F32),
            pltpu.VMEM((k, 4, 2, ROWS, F0), BF),
            pltpu.VMEM((k, 2, 2, 2, ROWS, f1), BF),
            pltpu.VMEM((k, 4, 2, ROWS, F0), BF),
            pltpu.VMEM((k, 4, 2, ROWS, f1), BF),
            pltpu.VMEM((k, 2, ROWS, F0), BF),
            pltpu.VMEM((k, 2, ROWS, f1), BF),
            pltpu.VMEM((k, 4, 2, ROWS, F0), BF),
            pltpu.VMEM((k, 4, 2, ROWS, f1), BF),
            pltpu.VMEM((k, 2, ROWS, F0), BF),
            pltpu.VMEM((k, 2, ROWS, f1), BF),
            pltpu.VMEM((k, 2, ROWS, F0), BF),
            pltpu.VMEM((k, 2, ROWS, f1), BF),
            pltpu.VMEM((k, 4, 2, ROWS, F0), BF),
            pltpu.VMEM((k, 2, 2, 2, ROWS, f1), BF),
            pltpu.VMEM((8, lats), F32),
            pltpu.VMEM((8, lats), F32),
            pltpu.VMEM((8, lats), F32),
            pltpu.VMEM((4, 8, lats), F32),
            pltpu.VMEM((8, lats), F32),
            pltpu.VMEM((8, lats), F32),
            pltpu.VMEM((features, k * 128), BF),
            pltpu.VMEM((features, k * 128), BF),
            pltpu.VMEM((features, lats), BF),
            pltpu.SemaphoreType.DMA((20,)),
            pltpu.SemaphoreType.DMA((messages,)),
            pltpu.SemaphoreType.DMA((9,)),
        ],
        compiler_params=pltpu.CompilerParams(
            collective_id=0, has_side_effects=True, vmem_limit_bytes=40 * 2**20
        ),
        name="crosscoder_step",
    )(*(pltpu.with_memory_space_constraint(a, pltpu.HBM) for a in operands))

    grad_encoder, grad_decoder = gradients(turned, pg.reshape(-1, lats), dgrad)
    return grad_encoder, grad_decoder.T


def gradients_kernel(turned, pg, dgrad, enc_grad, dec_grad, product, sems):
    copies = [pltpu.make_async_copy(dgrad, dec_grad, sems.at[0])]
    copies[0].start()
    pieces, size = product.shape[:2]
    for n in range(pieces):
        rows = pl.ds(n * size, size)
        product[n] = jnp.dot(turned[rows], pg[...], preferred_element_type=F32).astype(BF)
        copies.append(pltpu.make_async_copy(product.at[n], enc_grad.at[rows], sems.at[n + 1]))
        copies[-1].start()
    for copy in copies:
        copy.wait()


def gradients(turned, pg, dgrad):
    features, lats = dgrad.shape
    pieces = 3
    vmem = pl.BlockSpec(memory_space=pltpu.VMEM)
    memory = pl.BlockSpec(memory_space=pl.ANY)
    return pl.pallas_call(
        gradients_kernel,
        out_shape=[jax.ShapeDtypeStruct(dgrad.shape, BF)] * 2,
        in_specs=[vmem, vmem, memory],
        out_specs=[memory, memory],
        scratch_shapes=[
            pltpu.VMEM((pieces, features // pieces, lats), BF),
            pltpu.SemaphoreType.DMA((pieces + 1,)),
        ],
        compiler_params=pltpu.CompilerParams(vmem_limit_bytes=24 * 2**20),
        name="gradients",
    )(turned, pg, dgrad)


def solution(mesh):
    in_specs = (
        P(),
        P("latent", "layer"),
        P("layer", "latent"),
        P("latent"),
        P("latent", "layer"),
        P("layer"),
    )
    out_specs = (P("layer", "latent"), P("latent", "layer"))
    return jax.shard_map(shards, mesh=mesh, in_specs=in_specs, out_specs=out_specs, check_vma=False)
```

```python
import functools
import math

import jax
import jax.numpy as jnp
from jax import lax
from jax.experimental import pallas as pl
from jax.experimental.pallas import tpu as pltpu
from jax.sharding import PartitionSpec as P

D = 3584
LAYERS = 3
PENALTY = 0.3
ROWS = 16
F0 = 640
CHUNKS = 4
ORDER = (
    0, 1, 0, 0, 3, 2, 1, 1, 4, 0, 1, 2, 3, 3, 0, 0, 2, 1, 1, 3, 0,
    2, 5, 3, 1, 0, 3, 0, 1, 2, 3, 2, 0, 1, 0, 3, 2, 6, 1, 3, 1, 2,
    0, 7, 3, 2, 3, 1, 2, 2, 0, 8, 1, 3, 9, 2, 10, 3, 1, 3, 0, 2, 2,
)
MESH = pl.DeviceIdType.MESH
BF = jnp.bfloat16
F32 = jnp.float32


class Links:
    def __init__(self, send_sems, recv_sems, me):
        self.send_sems, self.recv_sems, self.me = send_sems, recv_sems, me
        self.names, self.families = {}, {}

    def copy(self, name, src, dst, device):
        i = self.names.setdefault(name, len(self.names))
        j = self.families.setdefault(name[0], len(self.families))
        return pltpu.make_async_remote_copy(
            src_ref=src,
            dst_ref=dst,
            send_sem=self.send_sems.at[j],
            recv_sem=self.recv_sems.at[i],
            device_id=device,
            device_id_type=MESH,
        )

    def send(self, name, src, dst, device):
        self.copy(name, src, dst, device).start()

    def recv(self, name, view):
        self.copy(name, view, view, self.me).wait_recv()

    def sent(self, family, view):
        i = self.families[family]
        pltpu.make_async_copy(view, view, self.send_sems.at[i]).wait()


class Ring:
    def __init__(self, place, device_at):
        self.place, self.device_at = place, device_at

    def at(self, shift):
        return lax.rem(self.place + shift % 4, 4)

    def device(self, shift):
        return self.device_at(self.at(shift))


def direct_start(links, tag, ring, source, target):
    for d in (2, 1, 3):
        links.send(tag, source(ring.at(d)), target(ring.at(0)), ring.device(d))


def kernel(
    scale,
    ids_hbm, bank_hbm, bias_hbm, dbias_hbm, enc_hbm, dec_hbm,
    turned_out, dgrad_out, pg_out,
    ids_ref, bank_ref, bias_ref, dbias_ref, enc, dec, blk0, blk1, bk0, bk1,
    parts, from_core, sums, zgot, lat, pg, slope,
    rp0, rp1, got0, got1, s0, s1, d0, d1, q0, q1, e0, e1, rs0, rs1,
    sq_part, sq_core, sq_chip, sq_z, norms_ref, coef_ref, turned, resid_turned, dgrad,
    send_sems, recv_sems, local_sems,
):
    layer, latent = lax.axis_index("layer"), lax.axis_index("latent")
    z, core = layer // 2, lax.rem(layer, 2)
    x, y = latent // 8, lax.rem(latent, 4)
    zl = lax.rem(latent // 4, 2)
    features = enc.shape[0]
    ring_z = Ring(z, lambda q: (q * 2 + core, latent))
    ring_x = Ring(x, lambda q: (layer, q * 8 + zl * 4 + y))
    ring_y = Ring(y, lambda q: (layer, x * 8 + zl * 4 + q))
    core_peer = (z * 2 + 1 - core, latent)
    zl_peer = (layer, x * 8 + (1 - zl) * 4 + y)
    links = Links(send_sems, recv_sems, (layer, latent))

    dec_copy = pltpu.make_async_copy(dec_hbm, dec, local_sems.at[0])
    enc_copy = pltpu.make_async_copy(enc_hbm, enc, local_sems.at[1])
    bank_copy = pltpu.make_async_copy(bank_hbm, bank_ref, local_sems.at[8])
    small_copies = [
        pltpu.make_async_copy(src, dst, local_sems.at[9 + i])
        for i, (src, dst) in enumerate(((ids_hbm, ids_ref), (bias_hbm, bias_ref), (dbias_hbm, dbias_ref)))
    ]
    for copy in (bank_copy, *small_copies, dec_copy, enc_copy):
        copy.start()

    partners = [core_peer, zl_peer]
    for ring in (ring_x, ring_y, ring_z):
        partners += [ring.device(d) for d in (1, 2, 3)]
    barrier = pltpu.get_barrier_semaphore()
    for device in partners:
        pl.semaphore_signal(barrier, inc=1, device_id=device, device_id_type=MESH)
    pl.semaphore_wait(barrier, len(partners))

    def counts(rows):
        hits = (ids_ref[...][None, :] == rows).astype(F32)
        return jnp.sum(hits, axis=1, keepdims=True)

    def bank_rows(k, block, n, stride=1):
        i = lax.broadcasted_iota(jnp.int32, (n, 1), 0)
        j = block + stride * (i // ROWS)
        at_x = j // 2
        at_y = 2 * lax.rem(j, 2) + lax.rem(at_x + k % 2, 2)
        return ((at_x * 2 + k // 2) * 4 + at_y) * ROWS + lax.rem(i, ROWS)

    def first(buf, k, q):
        return buf.at[k, q]

    def other(buf, k, q):
        return buf.at[k, :, lax.rem(q + k % 2, 2), q // 2]

    def bank_first(k, q):
        return bk0.at[k // 2, q, :, lax.rem(q + k % 2, 2)]

    def bank_other(k, q):
        return bk1.at[k // 2, :, lax.rem(q + k % 2, 2), q]

    def bank_spread(k):
        direct_start(links, ("b2", k), ring_x, lambda q: bank_first(k, x), lambda q: bank_first(k, q))
        direct_start(links, ("b3", k), ring_y, lambda q: bank_other(k, y), lambda q: bank_other(k, q))

    def bank_chunk(k):
        low, odd = k // 2, k % 2
        places = [(i, 2 * j + (i + odd) % 2) for i in range(4) for j in range(2)]
        b0 = [bk0[low, i, j // 2, j % 2] for i, j in places]
        b1 = [bk1[low, i // 2, i % 2, j] for i, j in places]
        return jnp.concatenate(b0, axis=0), jnp.concatenate(b1, axis=0)

    def product(s, k, left, weight):
        def tile(n, carry):
            at = pl.ds(pl.multiple_of(n * 256, 256), 256)
            out = jnp.dot(left[0], weight[:F0, at], preferred_element_type=F32)
            out += jnp.dot(left[1], weight[F0:, at], preferred_element_type=F32)
            parts[s, k, :, :, :, at] = out.astype(BF).reshape(2, 4, ROWS, 256)
            return carry

        lax.fori_loop(0, 4, tile, 0, unroll=True)
        links.send(("core", s, k), parts.at[s, k, 1 - core], from_core.at[s, k], core_peer)

    def z_scatter(s, k):
        links.recv(("core", s, k), from_core.at[s, k])
        own = parts[s, k, core].astype(F32) + from_core[s, k].astype(F32)
        sums[s, k] = own.astype(BF)
        direct_start(
            links, ("zs", s, k), ring_z, lambda q: sums.at[s, k, q], lambda q: zgot.at[s, k, q]
        )

    def z_sum(s, k):
        links.recv(("zs", s, k), zgot.at[s, k, pl.ds(0, 3)])
        total = sums[s, k, z].astype(F32)
        for shift in (1, 2, 3):
            total += zgot[s, k, ring_z.at(shift)].astype(F32)
        return total

    def to_core(s, k, buf, shift):
        block = buf.at[k, core, ring_z.at(shift)]
        links.send(("zc", s, k), block, block, core_peer)

    def z_gather(s, k, buf):
        own = buf.at[k, core, z]
        direct_start(links, ("zg", s, k), ring_z, lambda q: own, lambda q: buf.at[k, core, q])
        to_core(s, k, buf, 0)

    def z_pass(s, k, buf):
        links.recv(("zg", s, k), buf.at[k, core, pl.ds(0, 3)])
        for shift in (1, 2, 3):
            to_core(s, k, buf, shift)

    def z_finish(s, k, buf):
        links.recv(("zc", s, k), buf.at[k, 1 - core])

    def encode(k):
        links.recv(("b2", k), got0.at[k, pl.ds(0, 3)])
        links.recv(("b3", k), got1.at[k, pl.ds(0, 3)])
        product(0, k, bank_chunk(k), enc)

    def latents(k):
        pre = z_sum(0, k) + bias_ref[...][None, :]
        soft = jnp.maximum(pre, 0.0) + jnp.log1p(jnp.exp(-jnp.abs(pre)))
        lat[k, core, z] = soft.astype(BF)
        slope[k] = jax.nn.sigmoid(pre)
        z_gather(0, k, lat)

    def decode(k):
        z_finish(0, k, lat)
        rows = lat[k].reshape(128, -1)
        over = (((1,), (1,)), ((), ()))
        out = lax.dot_general(rows, dec[:F0], over, preferred_element_type=F32)
        rp0[k] = out.astype(BF).reshape(4, 2, ROWS, F0)
        direct_start(links, ("xs", k), ring_x, lambda q: first(rp0, k, q), lambda q: got0.at[k, q])
        out = lax.dot_general(rows, dec[F0:], over, preferred_element_type=F32)
        rp1[k] = out.astype(BF).reshape(2, 2, 2, ROWS, features - F0)
        direct_start(links, ("ys", k), ring_y, lambda q: other(rp1, k, q), lambda q: got1.at[k, q])

    def recon_second(k):
        for tag, ring, own, got, s, d, next_ring in (
            ("x", ring_x, first(rp0, k, x), got0, s0, d0, ring_y),
            ("y", ring_y, other(rp1, k, y), got1, s1, d1, ring_x),
        ):
            links.recv((tag + "s", k), got.at[k, pl.ds(0, 3)])
            total = own[...].astype(F32)
            for shift in (1, 2, 3):
                total += got[k, ring.at(shift)].astype(F32)
            s[k] = total.astype(BF)
            direct_start(links, (tag + "t", k), next_ring, lambda q: s.at[k], lambda q: d.at[k, q])

    def recon_third(k):
        for tag, ring, s, d, t, e in (("xt", ring_y, s0, d0, q0, e0), ("yt", ring_x, s1, d1, q1, e1)):
            links.recv((tag, k), d.at[k, pl.ds(0, 3)])
            total = s[k].astype(F32)
            for shift in (1, 2, 3):
                total += d[k, ring.at(shift)].astype(F32)
            t[k] = total.astype(BF)
            links.send((tag + "z", k), t.at[k], e.at[k], zl_peer)

    def residual(k):
        j = 2 * lax.rem(y + k % 2, 2) + y // 2
        for tag, at, t, e, inputs, out, rows in (
            ("xt", pl.ds(0, F0), q0, e0, bank_first(k, x), first(rs0, k, x), bank_rows(k, 2 * x, 32)),
            ("yt", pl.ds(F0, features - F0), q1, e1, bank_other(k, y), other(rs1, k, y), bank_rows(k, j, 32, 4)),
        ):
            links.recv((tag + "z", k), e.at[k])
            weight = counts(rows) * scale
            for b in (0, 1):
                recon = t[k, b].astype(F32) + e[k, b].astype(F32) + dbias_ref[at][None, :]
                value = recon - inputs[b].astype(F32)
                out[b] = (value * weight[b * ROWS : (b + 1) * ROWS]).astype(BF)
        direct_start(links, ("r2", k), ring_x, lambda q: first(rs0, k, x), lambda q: first(rs0, k, q))
        direct_start(links, ("r3", k), ring_y, lambda q: other(rs1, k, y), lambda q: other(rs1, k, q))

    def resid_chunk(k):
        return rs0[k].reshape(128, F0), rs1[k].reshape(128, features - F0)

    def backward(k):
        links.recv(("r2", k), got0.at[k, pl.ds(0, 3)])
        links.recv(("r3", k), got1.at[k, pl.ds(0, 3)])
        product(1, k, resid_chunk(k), dec)

    def latent_gradient(k):
        weight = counts(bank_rows(k, core * 4 + z, ROWS))
        total_norm = norms_ref[0:1] + norms_ref[1:2] + norms_ref[2:3]
        grad = z_sum(1, k) + weight * (PENALTY * scale * total_norm)
        pg[k, core, z] = (grad * slope[k]).astype(BF)
        z_gather(1, k, pg)

    def bank_send():
        bank_copy.wait()
        blk0[zl] = bank_ref[:, :F0]
        blk1[zl] = bank_ref[:, F0:]
        links.send(("bz0",), blk0.at[zl], blk0.at[zl], zl_peer)
        links.send(("bz1",), blk1.at[zl], blk1.at[zl], zl_peer)

    def bank_recv():
        links.recv(("bz0",), blk0.at[1 - zl])
        links.recv(("bz1",), blk1.at[1 - zl])
        for low in (0, 1):
            own0 = bk0.at[low, x, y // 2, lax.rem(y, 2)]
            own1 = bk1.at[low, x // 2, lax.rem(x, 2), y]
            own0[...] = blk0[low]
            own1[...] = blk1[low]
            direct_start(
                links, ("b0", low), ring_y, lambda q: own0, lambda q: bk0.at[low, x, q // 2, lax.rem(q, 2)]
            )
            direct_start(
                links, ("b1", low), ring_x, lambda q: own1, lambda q: bk1.at[low, q // 2, lax.rem(q, 2), y]
            )

    first_done = []

    def bank_second(k):
        if k // 2 not in first_done:
            first_done.append(k // 2)
            links.recv(("b0", k // 2), e0.at[pl.ds(0, 3), 0])
            links.recv(("b1", k // 2), e1.at[pl.ds(0, 3), 0])
        bank_spread(k)
        if k == 1:
            squares_send()
            squares_second()
            enc_copy.wait()

    def squares_send():
        for copy in (*small_copies, dec_copy):
            copy.wait()
        row = lax.broadcasted_iota(jnp.int32, (8, features), 0)
        column = lax.broadcasted_iota(jnp.int32, (8, features), 1) + layer * features
        owner = jnp.where((column >= row * D) & (column < (row + 1) * D), 1.0, 0.0).astype(BF)

        def square(n, carry):
            at = pl.ds(pl.multiple_of(n * 256, 256), 256)
            wide = dec[:, at].astype(F32)
            wide = wide * wide
            high = wide.astype(BF)
            low = (wide - high.astype(F32)).astype(BF)
            total = jnp.dot(owner, high, preferred_element_type=F32)
            total += jnp.dot(owner, low, preferred_element_type=F32)
            sq_part[:, at] = total
            return carry

        lax.fori_loop(0, 4, square, 0, unroll=True)
        links.send(("sqc",), sq_part, sq_core, core_peer)

    def squares_second():
        links.recv(("sqc",), sq_core)
        sq_chip[...] = sq_part[...] + sq_core[...]
        direct_start(links, ("sqz",), ring_z, lambda q: sq_chip, lambda q: sq_z.at[q])

    def squares_sum():
        links.recv(("sqz",), sq_z.at[pl.ds(0, 3)])
        squares = sq_chip[...]
        for shift in (1, 2, 3):
            squares += sq_z[ring_z.at(shift)]
        norms_ref[...] = jnp.sqrt(squares + 1e-6)

    def copy_out(i, src, dst):
        copy = pltpu.make_async_copy(src, dst, local_sems.at[i])
        copy.start()
        outgoing.append(copy)

    def coefficients():
        colsum = jnp.zeros((1, lat.shape[-1]), F32)
        for k in range(CHUNKS):
            weight = counts(bank_rows(k, 0, 128))
            colsum += jnp.sum(lat[k].reshape(128, -1).astype(F32) * weight, axis=0, keepdims=True)
        coef_ref[...] = (PENALTY * scale * colsum) / norms_ref[...]

    def turn(buf, chunk, k):
        at = pl.ds(128 * k, 128)
        b0, b1 = chunk(k)
        buf[:F0, at] = b0.T
        buf[F0:, at] = b1.T

    def decoder_gradient(first, last):
        feature = layer * features + lax.broadcasted_iota(jnp.int32, (features, 1), 0)

        def tile(n, carry):
            at = pl.ds(pl.multiple_of(n * 256, 256), 256)
            rows = lat[:, :, :, :, at].reshape(512, 256)
            out = jnp.dot(resid_turned[...], rows, preferred_element_type=F32)
            spread = jnp.where(
                feature < D, coef_ref[0:1, at], jnp.where(feature < 2 * D, coef_ref[1:2, at], coef_ref[2:3, at])
            )
            dgrad[:, at] = (out + spread * dec[:, at].astype(F32)).astype(BF)
            return carry

        lax.fori_loop(first, last, tile, 0)

    outgoing = []
    def finish_chunk(k):
        z_finish(1, k, pg)
        copy_out(4 + k, pg.at[k], pg_out.at[k])

    chunk_steps = (
        bank_second,
        encode,
        lambda k: z_scatter(0, k),
        latents,
        lambda k: z_pass(0, k, lat),
        decode,
        recon_second,
        recon_third,
        residual,
        backward,
        lambda k: z_scatter(1, k),
        latent_gradient,
        lambda k: z_pass(1, k, pg),
        finish_chunk,
    )

    def turn_bank(first, last):
        for k in (first, last):
            turn(turned, bank_chunk, k)
        if last == 3:
            copy_out(2, turned, turned_out)

    def turn_resid(first, last):
        for k in (first, last):
            turn(resid_turned, resid_chunk, k)

    def finish_decoder():
        decoder_gradient(2, 4)
        copy_out(3, dgrad, dgrad_out)

    once = (
        lambda: (squares_sum(), turn_bank(0, 1)),
        lambda: turn_bank(2, 3),
        coefficients,
        lambda: turn_resid(0, 1),
        lambda: turn_resid(2, 3),
        lambda: decoder_gradient(0, 2),
        finish_decoder,
    )
    steps = [(bank_send,), (bank_recv,)]
    left = [iter(chunk_steps) for k in range(CHUNKS)]
    for k in ORDER:
        steps.append((next(left[k]), k) if k < CHUNKS else (once[k - CHUNKS],))
    for step, *given in steps:
        step(*given)
    for family, view in (
        ("bz0", blk0.at[0]),
        ("bz1", blk1.at[0]),
        ("b0", e0.at[pl.ds(0, 3)]),
        ("b1", e1.at[pl.ds(0, 3)]),
        ("b2", got0.at[:, pl.ds(0, 3)]),
        ("b3", got1.at[:, pl.ds(0, 3)]),
        ("sqc", sq_part),
        ("sqz", sq_z.at[pl.ds(0, 3)]),
        ("core", sums),
        ("zs", zgot.at[:, :, pl.ds(0, 3)]),
        ("zg", zgot.at[:, :, pl.ds(0, 3)]),
        ("zc", sums),
        ("xs", got0.at[:, pl.ds(0, 3)]),
        ("ys", got1.at[:, pl.ds(0, 3)]),
        ("xt", got0.at[:, pl.ds(0, 3)]),
        ("yt", got1.at[:, pl.ds(0, 3)]),
        ("xtz", e0),
        ("ytz", e1),
        ("r2", got0.at[:, pl.ds(0, 3)]),
        ("r3", got1.at[:, pl.ds(0, 3)]),
    ):
        links.sent(family, view)
    for copy in outgoing:
        copy.wait()


def shards(ids, bank, enc_weight, enc_bias, dec_weight, dec_bias):
    tokens = ids.shape[0]
    features, lats = enc_weight.shape
    dec = dec_weight.T
    f1 = features - F0
    scale = 1.0 / math.sqrt(tokens)
    k = CHUNKS
    operands = (ids, bank, enc_bias, dec_bias, enc_weight, dec)
    messages = 80
    turned, dgrad, pg = pl.pallas_call(
        functools.partial(kernel, scale),
        out_shape=[
            jax.ShapeDtypeStruct((features, k * 128), BF),
            jax.ShapeDtypeStruct((features, lats), BF),
            jax.ShapeDtypeStruct((k, 2, 4, ROWS, lats), BF),
        ],
        in_specs=[pl.BlockSpec(memory_space=pl.ANY)] * 6,
        out_specs=[pl.BlockSpec(memory_space=pl.ANY)] * 3,
        scratch_shapes=[
            pltpu.VMEM(ids.shape, jnp.int32),
            pltpu.VMEM(bank.shape, BF),
            pltpu.VMEM(enc_bias.shape, F32),
            pltpu.VMEM(dec_bias.shape, F32),
            pltpu.VMEM((features, lats), BF),
            pltpu.VMEM((features, lats), BF),
            pltpu.VMEM((2, ROWS, F0), BF),
            pltpu.VMEM((2, ROWS, f1), BF),
            pltpu.VMEM((2, 4, 2, 2, ROWS, F0), BF),
            pltpu.VMEM((2, 2, 2, 4, ROWS, f1), BF),
            pltpu.VMEM((2, k, 2, 4, ROWS, lats), BF),
            pltpu.VMEM((2, k, 4, ROWS, lats), BF),
            pltpu.VMEM((2, k, 4, ROWS, lats), BF),
            pltpu.VMEM((2, k, 4, ROWS, lats), BF),
            pltpu.VMEM((k, 2, 4, ROWS, lats), BF),
            pltpu.VMEM((k, 2, 4, ROWS, lats), BF),
            pltpu.VMEM((k, ROWS, lats), F32),
            pltpu.VMEM((k, 4, 2, ROWS, F0), BF),
            pltpu.VMEM((k, 2, 2, 2, ROWS, f1), BF),
            pltpu.VMEM((k, 4, 2, ROWS, F0), BF),
            pltpu.VMEM((k, 4, 2, ROWS, f1), BF),
            pltpu.VMEM((k, 2, ROWS, F0), BF),
            pltpu.VMEM((k, 2, ROWS, f1), BF),
            pltpu.VMEM((k, 4, 2, ROWS, F0), BF),
            pltpu.VMEM((k, 4, 2, ROWS, f1), BF),
            pltpu.VMEM((k, 2, ROWS, F0), BF),
            pltpu.VMEM((k, 2, ROWS, f1), BF),
            pltpu.VMEM((k, 2, ROWS, F0), BF),
            pltpu.VMEM((k, 2, ROWS, f1), BF),
            pltpu.VMEM((k, 4, 2, ROWS, F0), BF),
            pltpu.VMEM((k, 2, 2, 2, ROWS, f1), BF),
            pltpu.VMEM((8, lats), F32),
            pltpu.VMEM((8, lats), F32),
            pltpu.VMEM((8, lats), F32),
            pltpu.VMEM((4, 8, lats), F32),
            pltpu.VMEM((8, lats), F32),
            pltpu.VMEM((8, lats), F32),
            pltpu.VMEM((features, k * 128), BF),
            pltpu.VMEM((features, k * 128), BF),
            pltpu.VMEM((features, lats), BF),
            pltpu.SemaphoreType.DMA((20,)),
            pltpu.SemaphoreType.DMA((messages,)),
            pltpu.SemaphoreType.DMA((12,)),
        ],
        compiler_params=pltpu.CompilerParams(
            collective_id=0, has_side_effects=True, vmem_limit_bytes=40 * 2**20
        ),
        name="crosscoder_step",
    )(*(pltpu.with_memory_space_constraint(a, pltpu.HBM) for a in operands))

    grad_encoder, grad_decoder = gradients(turned, pg.reshape(-1, lats), dgrad)
    return grad_encoder, grad_decoder.T


def gradients_kernel(turned, pg, dgrad, enc_grad, dec_grad, product, sems):
    copies = [pltpu.make_async_copy(dgrad, dec_grad, sems.at[0])]
    copies[0].start()
    pieces, size = product.shape[:2]
    for n in range(pieces):
        rows = pl.ds(n * size, size)
        product[n] = jnp.dot(turned[rows], pg[...], preferred_element_type=F32).astype(BF)
        copies.append(pltpu.make_async_copy(product.at[n], enc_grad.at[rows], sems.at[n + 1]))
        copies[-1].start()
    for copy in copies:
        copy.wait()


def gradients(turned, pg, dgrad):
    features, lats = dgrad.shape
    pieces = 3
    vmem = pl.BlockSpec(memory_space=pltpu.VMEM)
    memory = pl.BlockSpec(memory_space=pl.ANY)
    return pl.pallas_call(
        gradients_kernel,
        out_shape=[jax.ShapeDtypeStruct(dgrad.shape, BF)] * 2,
        in_specs=[vmem, vmem, memory],
        out_specs=[memory, memory],
        scratch_shapes=[
            pltpu.VMEM((pieces, features // pieces, lats), BF),
            pltpu.SemaphoreType.DMA((pieces + 1,)),
        ],
        compiler_params=pltpu.CompilerParams(vmem_limit_bytes=24 * 2**20),
        name="gradients",
    )(turned, pg, dgrad)


def solution(mesh):
    in_specs = (
        P(),
        P("latent", "layer"),
        P("layer", "latent"),
        P("latent"),
        P("latent", "layer"),
        P("layer"),
    )
    out_specs = (P("layer", "latent"), P("latent", "layer"))
    return jax.shard_map(shards, mesh=mesh, in_specs=in_specs, out_specs=out_specs, check_vma=False)
```

```python
import functools
import math

import jax
import jax.numpy as jnp
from jax import lax
from jax.experimental import pallas as pl
from jax.experimental.pallas import tpu as pltpu
from jax.sharding import PartitionSpec as P

D = 3584
LAYERS = 3
PENALTY = 0.3
ROWS = 16
F0 = 640
CHUNKS = 4
ORDER = (
    0, 1, 2, 0, 3, 0, 1, 1, 2, 0, 1, 3, 3, 2, 4, 5, 0, 0, 1, 1, 3,
    0, 2, 1, 0, 3, 3, 2, 0, 1, 2, 6, 3, 0, 2, 0, 3, 1, 2, 3, 0, 1,
    2, 1, 3, 3, 2, 7, 8, 2, 9, 1, 0, 3, 2, 10, 1, 0, 3, 2, 1, 3, 2,
)
MESH = pl.DeviceIdType.MESH
BF = jnp.bfloat16
F32 = jnp.float32


class Links:
    def __init__(self, send_sems, recv_sems, me):
        self.send_sems, self.recv_sems, self.me = send_sems, recv_sems, me
        self.names, self.families = {}, {}

    def copy(self, name, src, dst, device):
        i = self.names.setdefault(name, len(self.names))
        j = self.families.setdefault(name[0], len(self.families))
        return pltpu.make_async_remote_copy(
            src_ref=src,
            dst_ref=dst,
            send_sem=self.send_sems.at[j],
            recv_sem=self.recv_sems.at[i],
            device_id=device,
            device_id_type=MESH,
        )

    def send(self, name, src, dst, device):
        self.copy(name, src, dst, device).start()

    def recv(self, name, view):
        self.copy(name, view, view, self.me).wait_recv()

    def sent(self, family, view):
        i = self.families[family]
        pltpu.make_async_copy(view, view, self.send_sems.at[i]).wait()


class Ring:
    def __init__(self, place, device_at):
        self.place, self.device_at = place, device_at

    def at(self, shift):
        return lax.rem(self.place + shift % 4, 4)

    def device(self, shift):
        return self.device_at(self.at(shift))


def direct_start(links, tag, ring, source, target):
    for d in (2, 1, 3):
        links.send(tag, source(ring.at(d)), target(ring.at(0)), ring.device(d))


def kernel(
    scale,
    ids_hbm, bank_hbm, bias_hbm, dbias_hbm, enc_hbm, dec_hbm,
    turned_out, dgrad_out, pg_out,
    ids_ref, bank_ref, bias_ref, dbias_ref, enc, dec, blk0, blk1, bk0, bk1,
    parts, from_core, sums, zgot, lat, pg, slope,
    rp0, rp1, got0, got1, s0, s1, d0, d1, q0, q1, e0, e1, rs0, rs1,
    sq_part, sq_core, sq_chip, sq_z, norms_ref, coef_ref, turned, resid_turned, dgrad,
    send_sems, recv_sems, local_sems,
):
    layer, latent = lax.axis_index("layer"), lax.axis_index("latent")
    z, core = layer // 2, lax.rem(layer, 2)
    x, y = latent // 8, lax.rem(latent, 4)
    zl = lax.rem(latent // 4, 2)
    features = enc.shape[0]
    ring_z = Ring(z, lambda q: (q * 2 + core, latent))
    ring_x = Ring(x, lambda q: (layer, q * 8 + zl * 4 + y))
    ring_y = Ring(y, lambda q: (layer, x * 8 + zl * 4 + q))
    core_peer = (z * 2 + 1 - core, latent)
    zl_peer = (layer, x * 8 + (1 - zl) * 4 + y)
    links = Links(send_sems, recv_sems, (layer, latent))

    dec_copy = pltpu.make_async_copy(dec_hbm, dec, local_sems.at[0])
    enc_copy = pltpu.make_async_copy(enc_hbm, enc, local_sems.at[1])
    bank_copy = pltpu.make_async_copy(bank_hbm, bank_ref, local_sems.at[8])
    small_copies = [
        pltpu.make_async_copy(src, dst, local_sems.at[9 + i])
        for i, (src, dst) in enumerate(((ids_hbm, ids_ref), (bias_hbm, bias_ref), (dbias_hbm, dbias_ref)))
    ]
    for copy in (bank_copy, *small_copies, dec_copy, enc_copy):
        copy.start()

    partners = [core_peer, zl_peer]
    for ring in (ring_x, ring_y, ring_z):
        partners += [ring.device(d) for d in (1, 2, 3)]
    barrier = pltpu.get_barrier_semaphore()
    for device in partners:
        pl.semaphore_signal(barrier, inc=1, device_id=device, device_id_type=MESH)
    pl.semaphore_wait(barrier, len(partners))

    def counts(rows):
        hits = (ids_ref[...][None, :] == rows).astype(F32)
        return jnp.sum(hits, axis=1, keepdims=True)

    def bank_rows(k, block, n, stride=1):
        i = lax.broadcasted_iota(jnp.int32, (n, 1), 0)
        j = block + stride * (i // ROWS)
        at_x = j // 2
        at_y = 2 * lax.rem(j, 2) + lax.rem(at_x + k % 2, 2)
        return ((at_x * 2 + k // 2) * 4 + at_y) * ROWS + lax.rem(i, ROWS)

    def first(buf, k, q):
        return buf.at[k, q]

    def other(buf, k, q):
        return buf.at[k, :, lax.rem(q + k % 2, 2), q // 2]

    def bank_first(k, q):
        return bk0.at[k // 2, q, :, lax.rem(q + k % 2, 2)]

    def bank_other(k, q):
        return bk1.at[k // 2, :, lax.rem(q + k % 2, 2), q]

    def bank_spread(k):
        direct_start(links, ("b2", k), ring_x, lambda q: bank_first(k, x), lambda q: bank_first(k, q))
        direct_start(links, ("b3", k), ring_y, lambda q: bank_other(k, y), lambda q: bank_other(k, q))

    def bank_chunk(k):
        low, odd = k // 2, k % 2
        places = [(i, 2 * j + (i + odd) % 2) for i in range(4) for j in range(2)]
        b0 = [bk0[low, i, j // 2, j % 2] for i, j in places]
        b1 = [bk1[low, i // 2, i % 2, j] for i, j in places]
        return jnp.concatenate(b0, axis=0), jnp.concatenate(b1, axis=0)

    def product(s, k, left, weight):
        def tile(n, carry):
            at = pl.ds(pl.multiple_of(n * 256, 256), 256)
            out = jnp.dot(left[0], weight[:F0, at], preferred_element_type=F32)
            out += jnp.dot(left[1], weight[F0:, at], preferred_element_type=F32)
            parts[s, k, :, :, :, at] = out.astype(BF).reshape(2, 4, ROWS, 256)
            return carry

        lax.fori_loop(0, 4, tile, 0, unroll=True)
        links.send(("core", s, k), parts.at[s, k, 1 - core], from_core.at[s, k], core_peer)

    def z_scatter(s, k):
        links.recv(("core", s, k), from_core.at[s, k])
        own = parts[s, k, core].astype(F32) + from_core[s, k].astype(F32)
        sums[s, k] = own.astype(BF)
        direct_start(
            links, ("zs", s, k), ring_z, lambda q: sums.at[s, k, q], lambda q: zgot.at[s, k, q]
        )

    def z_sum(s, k):
        links.recv(("zs", s, k), zgot.at[s, k, pl.ds(0, 3)])
        total = sums[s, k, z].astype(F32)
        for shift in (1, 2, 3):
            total += zgot[s, k, ring_z.at(shift)].astype(F32)
        return total

    def to_core(s, k, buf, shift):
        block = buf.at[k, core, ring_z.at(shift)]
        links.send(("zc", s, k), block, block, core_peer)

    def z_gather(s, k, buf):
        own = buf.at[k, core, z]
        direct_start(links, ("zg", s, k), ring_z, lambda q: own, lambda q: buf.at[k, core, q])
        to_core(s, k, buf, 0)

    def z_pass(s, k, buf):
        links.recv(("zg", s, k), buf.at[k, core, pl.ds(0, 3)])
        for shift in (1, 2, 3):
            to_core(s, k, buf, shift)

    def z_finish(s, k, buf):
        links.recv(("zc", s, k), buf.at[k, 1 - core])

    def encode(k):
        links.recv(("b2", k), got0.at[k, pl.ds(0, 3)])
        links.recv(("b3", k), got1.at[k, pl.ds(0, 3)])
        product(0, k, bank_chunk(k), enc)

    def latents(k):
        pre = z_sum(0, k) + bias_ref[...][None, :]
        soft = jnp.maximum(pre, 0.0) + jnp.log1p(jnp.exp(-jnp.abs(pre)))
        lat[k, core, z] = soft.astype(BF)
        slope[k] = jax.nn.sigmoid(pre)
        z_gather(0, k, lat)

    def decode(k):
        z_finish(0, k, lat)
        rows = lat[k].reshape(128, -1)
        over = (((1,), (1,)), ((), ()))
        out = lax.dot_general(rows, dec[:F0], over, preferred_element_type=F32)
        rp0[k] = out.astype(BF).reshape(4, 2, ROWS, F0)
        direct_start(links, ("xs", k), ring_x, lambda q: first(rp0, k, q), lambda q: got0.at[k, q])
        out = lax.dot_general(rows, dec[F0:], over, preferred_element_type=F32)
        rp1[k] = out.astype(BF).reshape(2, 2, 2, ROWS, features - F0)
        direct_start(links, ("ys", k), ring_y, lambda q: other(rp1, k, q), lambda q: got1.at[k, q])

    def recon_second(k):
        for tag, ring, own, got, s, d, next_ring in (
            ("x", ring_x, first(rp0, k, x), got0, s0, d0, ring_y),
            ("y", ring_y, other(rp1, k, y), got1, s1, d1, ring_x),
        ):
            links.recv((tag + "s", k), got.at[k, pl.ds(0, 3)])
            total = own[...].astype(F32)
            for shift in (1, 2, 3):
                total += got[k, ring.at(shift)].astype(F32)
            s[k] = total.astype(BF)
            direct_start(links, (tag + "t", k), next_ring, lambda q: s.at[k], lambda q: d.at[k, q])

    def recon_third(k):
        for tag, ring, s, d, t, e in (("xt", ring_y, s0, d0, q0, e0), ("yt", ring_x, s1, d1, q1, e1)):
            links.recv((tag, k), d.at[k, pl.ds(0, 3)])
            total = s[k].astype(F32)
            for shift in (1, 2, 3):
                total += d[k, ring.at(shift)].astype(F32)
            t[k] = total.astype(BF)
            links.send((tag + "z", k), t.at[k], e.at[k], zl_peer)

    def residual(k):
        j = 2 * lax.rem(y + k % 2, 2) + y // 2
        for tag, at, t, e, inputs, out, rows in (
            ("xt", pl.ds(0, F0), q0, e0, bank_first(k, x), first(rs0, k, x), bank_rows(k, 2 * x, 32)),
            ("yt", pl.ds(F0, features - F0), q1, e1, bank_other(k, y), other(rs1, k, y), bank_rows(k, j, 32, 4)),
        ):
            links.recv((tag + "z", k), e.at[k])
            weight = counts(rows) * scale
            for b in (0, 1):
                recon = t[k, b].astype(F32) + e[k, b].astype(F32) + dbias_ref[at][None, :]
                value = recon - inputs[b].astype(F32)
                out[b] = (value * weight[b * ROWS : (b + 1) * ROWS]).astype(BF)
        direct_start(links, ("r2", k), ring_x, lambda q: first(rs0, k, x), lambda q: first(rs0, k, q))
        direct_start(links, ("r3", k), ring_y, lambda q: other(rs1, k, y), lambda q: other(rs1, k, q))

    def resid_chunk(k):
        return rs0[k].reshape(128, F0), rs1[k].reshape(128, features - F0)

    def backward(k):
        links.recv(("r2", k), got0.at[k, pl.ds(0, 3)])
        links.recv(("r3", k), got1.at[k, pl.ds(0, 3)])
        product(1, k, resid_chunk(k), dec)

    def latent_gradient(k):
        weight = counts(bank_rows(k, core * 4 + z, ROWS))
        total_norm = norms_ref[0:1] + norms_ref[1:2] + norms_ref[2:3]
        grad = z_sum(1, k) + weight * (PENALTY * scale * total_norm)
        pg[k, core, z] = (grad * slope[k]).astype(BF)
        z_gather(1, k, pg)

    def bank_send():
        bank_copy.wait()
        blk0[zl] = bank_ref[:, :F0]
        blk1[zl] = bank_ref[:, F0:]
        links.send(("bz0",), blk0.at[zl], blk0.at[zl], zl_peer)
        links.send(("bz1",), blk1.at[zl], blk1.at[zl], zl_peer)

    def bank_recv():
        links.recv(("bz0",), blk0.at[1 - zl])
        links.recv(("bz1",), blk1.at[1 - zl])
        for low in (0, 1):
            own0 = bk0.at[low, x, y // 2, lax.rem(y, 2)]
            own1 = bk1.at[low, x // 2, lax.rem(x, 2), y]
            own0[...] = blk0[low]
            own1[...] = blk1[low]
            direct_start(
                links, ("b0", low), ring_y, lambda q: own0, lambda q: bk0.at[low, x, q // 2, lax.rem(q, 2)]
            )
            direct_start(
                links, ("b1", low), ring_x, lambda q: own1, lambda q: bk1.at[low, q // 2, lax.rem(q, 2), y]
            )

    first_done = []

    def bank_second(k):
        if k // 2 not in first_done:
            first_done.append(k // 2)
            links.recv(("b0", k // 2), e0.at[pl.ds(0, 3), 0])
            links.recv(("b1", k // 2), e1.at[pl.ds(0, 3), 0])
        bank_spread(k)
        if k == 1:
            squares_send()
            squares_second()
            enc_copy.wait()

    def squares_send():
        for copy in (*small_copies, dec_copy):
            copy.wait()
        row = lax.broadcasted_iota(jnp.int32, (8, features), 0)
        column = lax.broadcasted_iota(jnp.int32, (8, features), 1) + layer * features
        owner = jnp.where((column >= row * D) & (column < (row + 1) * D), 1.0, 0.0).astype(BF)

        def square(n, carry):
            at = pl.ds(pl.multiple_of(n * 256, 256), 256)
            wide = dec[:, at].astype(F32)
            wide = wide * wide
            high = wide.astype(BF)
            low = (wide - high.astype(F32)).astype(BF)
            total = jnp.dot(owner, high, preferred_element_type=F32)
            total += jnp.dot(owner, low, preferred_element_type=F32)
            sq_part[:, at] = total
            return carry

        lax.fori_loop(0, 4, square, 0, unroll=True)
        links.send(("sqc",), sq_part, sq_core, core_peer)

    def squares_second():
        links.recv(("sqc",), sq_core)
        total = sq_part[...] + sq_core[...]
        for l in range(LAYERS):
            for g in range(8):
                sq_chip[g : g + 1, 128 * l : 128 * l + 128] = total[l : l + 1, 128 * g : 128 * g + 128]
        direct_start(links, ("sqz",), ring_z, lambda q: sq_chip, lambda q: sq_z.at[q])

    def squares_sum():
        links.recv(("sqz",), sq_z.at[pl.ds(0, 3)])
        squares = sq_chip[...]
        for shift in (1, 2, 3):
            squares += sq_z[ring_z.at(shift)]
        norms = jnp.sqrt(squares + 1e-6)
        norms_ref[...] = jnp.ones(norms_ref.shape, F32)
        for l in range(LAYERS):
            for g in range(8):
                norms_ref[l : l + 1, 128 * g : 128 * g + 128] = norms[g : g + 1, 128 * l : 128 * l + 128]

    def copy_out(i, src, dst):
        copy = pltpu.make_async_copy(src, dst, local_sems.at[i])
        copy.start()
        outgoing.append(copy)

    def coefficients():
        colsum = jnp.zeros((1, lat.shape[-1]), F32)
        for k in range(CHUNKS):
            weight = counts(bank_rows(k, 0, 128))
            colsum += jnp.sum(lat[k].reshape(128, -1).astype(F32) * weight, axis=0, keepdims=True)
        coef_ref[...] = (PENALTY * scale * colsum) / norms_ref[...]

    def turn(buf, chunk, k):
        at = pl.ds(128 * k, 128)
        b0, b1 = chunk(k)
        buf[:F0, at] = b0.T
        buf[F0:, at] = b1.T

    def decoder_gradient(first, last):
        feature = layer * features + lax.broadcasted_iota(jnp.int32, (features, 1), 0)

        def tile(n, carry):
            at = pl.ds(pl.multiple_of(n * 256, 256), 256)
            rows = lat[:, :, :, :, at].reshape(512, 256)
            out = jnp.dot(resid_turned[...], rows, preferred_element_type=F32)
            spread = jnp.where(
                feature < D, coef_ref[0:1, at], jnp.where(feature < 2 * D, coef_ref[1:2, at], coef_ref[2:3, at])
            )
            dgrad[:, at] = (out + spread * dec[:, at].astype(F32)).astype(BF)
            return carry

        lax.fori_loop(first, last, tile, 0)

    outgoing = []
    def finish_chunk(k):
        z_finish(1, k, pg)
        copy_out(4 + k, pg.at[k], pg_out.at[k])

    chunk_steps = (
        bank_second,
        encode,
        lambda k: z_scatter(0, k),
        latents,
        lambda k: z_pass(0, k, lat),
        decode,
        recon_second,
        recon_third,
        residual,
        backward,
        lambda k: z_scatter(1, k),
        latent_gradient,
        lambda k: z_pass(1, k, pg),
        finish_chunk,
    )

    def turn_bank(first, last):
        for k in (first, last):
            turn(turned, bank_chunk, k)
        if last == 3:
            copy_out(2, turned, turned_out)

    def turn_resid(first, last):
        for k in (first, last):
            turn(resid_turned, resid_chunk, k)

    def finish_decoder():
        decoder_gradient(2, 4)
        copy_out(3, dgrad, dgrad_out)

    once = (
        lambda: (squares_sum(), turn_bank(0, 1)),
        lambda: turn_bank(2, 3),
        coefficients,
        lambda: turn_resid(0, 1),
        lambda: turn_resid(2, 3),
        lambda: decoder_gradient(0, 2),
        finish_decoder,
    )
    steps = [(bank_send,), (bank_recv,)]
    left = [iter(chunk_steps) for k in range(CHUNKS)]
    for k in ORDER:
        steps.append((next(left[k]), k) if k < CHUNKS else (once[k - CHUNKS],))
    for step, *given in steps:
        step(*given)
    for family, view in (
        ("bz0", blk0.at[0]),
        ("bz1", blk1.at[0]),
        ("b0", e0.at[pl.ds(0, 3)]),
        ("b1", e1.at[pl.ds(0, 3)]),
        ("b2", got0.at[:, pl.ds(0, 3)]),
        ("b3", got1.at[:, pl.ds(0, 3)]),
        ("sqc", sq_part),
        ("sqz", sq_z.at[pl.ds(0, 3)]),
        ("core", sums),
        ("zs", zgot.at[:, :, pl.ds(0, 3)]),
        ("zg", zgot.at[:, :, pl.ds(0, 3)]),
        ("zc", sums),
        ("xs", got0.at[:, pl.ds(0, 3)]),
        ("ys", got1.at[:, pl.ds(0, 3)]),
        ("xt", got0.at[:, pl.ds(0, 3)]),
        ("yt", got1.at[:, pl.ds(0, 3)]),
        ("xtz", e0),
        ("ytz", e1),
        ("r2", got0.at[:, pl.ds(0, 3)]),
        ("r3", got1.at[:, pl.ds(0, 3)]),
    ):
        links.sent(family, view)
    for copy in outgoing:
        copy.wait()


def shards(ids, bank, enc_weight, enc_bias, dec_weight, dec_bias):
    tokens = ids.shape[0]
    features, lats = enc_weight.shape
    dec = dec_weight.T
    f1 = features - F0
    scale = 1.0 / math.sqrt(tokens)
    k = CHUNKS
    operands = (ids, bank, enc_bias, dec_bias, enc_weight, dec)
    messages = 80
    turned, dgrad, pg = pl.pallas_call(
        functools.partial(kernel, scale),
        out_shape=[
            jax.ShapeDtypeStruct((features, k * 128), BF),
            jax.ShapeDtypeStruct((features, lats), BF),
            jax.ShapeDtypeStruct((k, 2, 4, ROWS, lats), BF),
        ],
        in_specs=[pl.BlockSpec(memory_space=pl.ANY)] * 6,
        out_specs=[pl.BlockSpec(memory_space=pl.ANY)] * 3,
        scratch_shapes=[
            pltpu.VMEM(ids.shape, jnp.int32),
            pltpu.VMEM(bank.shape, BF),
            pltpu.VMEM(enc_bias.shape, F32),
            pltpu.VMEM(dec_bias.shape, F32),
            pltpu.VMEM((features, lats), BF),
            pltpu.VMEM((features, lats), BF),
            pltpu.VMEM((2, ROWS, F0), BF),
            pltpu.VMEM((2, ROWS, f1), BF),
            pltpu.VMEM((2, 4, 2, 2, ROWS, F0), BF),
            pltpu.VMEM((2, 2, 2, 4, ROWS, f1), BF),
            pltpu.VMEM((2, k, 2, 4, ROWS, lats), BF),
            pltpu.VMEM((2, k, 4, ROWS, lats), BF),
            pltpu.VMEM((2, k, 4, ROWS, lats), BF),
            pltpu.VMEM((2, k, 4, ROWS, lats), BF),
            pltpu.VMEM((k, 2, 4, ROWS, lats), BF),
            pltpu.VMEM((k, 2, 4, ROWS, lats), BF),
            pltpu.VMEM((k, ROWS, lats), F32),
            pltpu.VMEM((k, 4, 2, ROWS, F0), BF),
            pltpu.VMEM((k, 2, 2, 2, ROWS, f1), BF),
            pltpu.VMEM((k, 4, 2, ROWS, F0), BF),
            pltpu.VMEM((k, 4, 2, ROWS, f1), BF),
            pltpu.VMEM((k, 2, ROWS, F0), BF),
            pltpu.VMEM((k, 2, ROWS, f1), BF),
            pltpu.VMEM((k, 4, 2, ROWS, F0), BF),
            pltpu.VMEM((k, 4, 2, ROWS, f1), BF),
            pltpu.VMEM((k, 2, ROWS, F0), BF),
            pltpu.VMEM((k, 2, ROWS, f1), BF),
            pltpu.VMEM((k, 2, ROWS, F0), BF),
            pltpu.VMEM((k, 2, ROWS, f1), BF),
            pltpu.VMEM((k, 4, 2, ROWS, F0), BF),
            pltpu.VMEM((k, 2, 2, 2, ROWS, f1), BF),
            pltpu.VMEM((8, lats), F32),
            pltpu.VMEM((8, lats), F32),
            pltpu.VMEM((8, 128 * LAYERS), F32),
            pltpu.VMEM((4, 8, 128 * LAYERS), F32),
            pltpu.VMEM((8, lats), F32),
            pltpu.VMEM((8, lats), F32),
            pltpu.VMEM((features, k * 128), BF),
            pltpu.VMEM((features, k * 128), BF),
            pltpu.VMEM((features, lats), BF),
            pltpu.SemaphoreType.DMA((20,)),
            pltpu.SemaphoreType.DMA((messages,)),
            pltpu.SemaphoreType.DMA((12,)),
        ],
        compiler_params=pltpu.CompilerParams(
            collective_id=0, has_side_effects=True, vmem_limit_bytes=40 * 2**20
        ),
        name="crosscoder_step",
    )(*(pltpu.with_memory_space_constraint(a, pltpu.HBM) for a in operands))

    grad_encoder, grad_decoder = gradients(turned, pg.reshape(-1, lats), dgrad)
    return grad_encoder, grad_decoder.T


def gradients_kernel(turned, pg, dgrad, enc_grad, dec_grad, product, sems):
    copies = [pltpu.make_async_copy(dgrad, dec_grad, sems.at[0])]
    copies[0].start()
    pieces, size = product.shape[:2]
    for n in range(pieces):
        rows = pl.ds(n * size, size)
        product[n] = jnp.dot(turned[rows], pg[...], preferred_element_type=F32).astype(BF)
        copies.append(pltpu.make_async_copy(product.at[n], enc_grad.at[rows], sems.at[n + 1]))
        copies[-1].start()
    for copy in copies:
        copy.wait()


def gradients(turned, pg, dgrad):
    features, lats = dgrad.shape
    pieces = 3
    vmem = pl.BlockSpec(memory_space=pltpu.VMEM)
    memory = pl.BlockSpec(memory_space=pl.ANY)
    return pl.pallas_call(
        gradients_kernel,
        out_shape=[jax.ShapeDtypeStruct(dgrad.shape, BF)] * 2,
        in_specs=[vmem, vmem, memory],
        out_specs=[memory, memory],
        scratch_shapes=[
            pltpu.VMEM((pieces, features // pieces, lats), BF),
            pltpu.SemaphoreType.DMA((pieces + 1,)),
        ],
        compiler_params=pltpu.CompilerParams(vmem_limit_bytes=24 * 2**20),
        name="gradients",
    )(turned, pg, dgrad)


def solution(mesh):
    in_specs = (
        P(),
        P("latent", "layer"),
        P("layer", "latent"),
        P("latent"),
        P("latent", "layer"),
        P("layer"),
    )
    out_specs = (P("layer", "latent"), P("latent", "layer"))
    return jax.shard_map(shards, mesh=mesh, in_specs=in_specs, out_specs=out_specs, check_vma=False)
```
